32 devices in a mesh: pb: 8 (over z, y), ka: 4 (over x, core).
Axes of the slice: x: 2, y: 2, z: 4, core: 2. Of those that a mesh axis runs over, the one named last changes fastest.
Arguments:
- queries: bfloat16 [2048, 4096], P('pb', 'ka'), may hold values from -25 to 25
- output_gradient: bfloat16 [2048, 4096], P('pb', 'ka'), may hold values from -6 to 6
- key_states: bfloat16 [2048, 2048], P(('pb', 'ka')), may hold values from -6 to 6
- value_inputs: bfloat16 [2048, 2048], P(('pb', 'ka')), may hold values from -6 to 6
- turn_ids: int32 [2048], replicated, may hold values from 0 to 3, never falling along the last dimension, each value on 1 to 1792 neighbouring positions
- listed: int32 [2, 16, 14], replicated, may hold values 0 or 1
Outputs:
- grad_queries: float32 [2048, 4096], P('pb', 'ka')
- grad_keys: float32 [2048, 2048], P(('pb', 'ka'))
- grad_values: float32 [2048, 2048], P(('pb', 'ka'))
The draws below stay inside these ranges and needn't reach their ends.
Inputs may be any that keep to these rules, and one draw needn't show every extreme that they name: `turn_ids`: turn numbers never fall along the window; every turn spans 1 to 1792 positions, and some turn spans exactly 1792.
All inputs are finite; a program needn't handle non-finite values.
Results may differ from the reference program's by a relative error of at most 0.003.
Values may be sent and summed in bfloat16 or wider, within the bound.
A program may use at most 128 MiB of HBM per device.

```python
import math
import jax
import jax.numpy as jnp
import numpy as np
from jax import lax

QUERY_HEADS = 32
KEY_VALUE_HEADS = 16
HEAD_SIZE = 128
HEAD_GROUPS = 2
BLOCK_POSITIONS = 128
BACK = 14
WINDOW_TOKENS = 2048
NB = 16


def shared_rows(key):
    pick_key, sign_key, power_key = jax.random.split(key, 3)
    chosen = jax.random.bernoulli(pick_key, 1.0 / 64.0, (WINDOW_TOKENS,))
    sign_rows = jnp.where(jax.random.bernoulli(sign_key, 0.5, (WINDOW_TOKENS, HEAD_SIZE)), 1.0, -1.0)
    strength = jax.random.uniform(power_key, (WINDOW_TOKENS,), minval=6.5, maxval=25.0)
    return (chosen, sign_rows, strength)


def draw_queries(key, part):
    self_key = jax.random.fold_in(key, 11)
    regular_portion = jnp.clip(jax.random.normal(self_key, (WINDOW_TOKENS, QUERY_HEADS * HEAD_SIZE), jnp.float32), -5.0, 5.0)
    chosen, sign_rows, strength = shared_rows(key)
    aligned = jnp.tile(strength[:, None] * sign_rows, (1, QUERY_HEADS))
    scaled = regular_portion
    drawn = jnp.where(chosen[:, None], aligned, scaled)
    return drawn.astype(jnp.bfloat16)


def draw_key_states(key, part):
    self_key = jax.random.fold_in(key, 23)
    regular_portion = jnp.clip(jax.random.normal(self_key, (WINDOW_TOKENS, KEY_VALUE_HEADS * HEAD_SIZE), jnp.float32), -5.0, 5.0)
    chosen, sign_rows, strength = shared_rows(key)
    magnitude = min(6.0, 192.0 / HEAD_SIZE)
    next_chosen = jnp.roll(chosen, -1)
    next_signs = jnp.roll(sign_rows, -1, axis=0)
    next_strength = jnp.roll(strength, -1)
    near_rows = magnitude * next_signs * (1.0 - 0.125 / next_strength)[:, None]
    exact_rows = magnitude * sign_rows
    value_per_head = jnp.where(chosen[:, None], exact_rows, near_rows)
    repeated_rows = jnp.tile(value_per_head, (1, KEY_VALUE_HEADS))
    scaled = regular_portion
    drawn = jnp.where((chosen | next_chosen)[:, None], repeated_rows, scaled)
    return drawn.astype(jnp.bfloat16)


def with_ends(values, own_key, smallest, high):
    longest = values.shape.index(max(values.shape))
    spots = []
    for shift in (0, 1):
        where = [jax.random.randint(jax.random.fold_in(own_key, axis), (), 0, length) for axis, length in enumerate(values.shape)]
        where[longest] = (where[longest] + shift) % values.shape[longest]
        spots.append(tuple(where))
    return values.at[spots[0]].set(smallest).at[spots[1]].set(high)


def block_levels(rng, extent, cuts, smallest, largest):
    loudness = 1.0
    for dim, parts in cuts:
        draws = jax.random.uniform(jax.random.fold_in(jax.random.fold_in(rng, 6), dim), (parts,), jnp.float32, smallest / len(cuts), largest / len(cuts))
        loudness = loudness * jnp.repeat(jnp.exp(draws), extent[dim] // parts).reshape((-1,) + (1,) * (len(extent) - 1 - dim))
    return loudness


def split_up(count, total, limit, lean):
    portions = [(1 << 20) // math.isqrt(grade ** lean) + 1 for grade in range(2, count + 1)]
    rest, holding = total - limit - (count - 1), [1] * (count - 1)
    while rest > 0:
        free = [i for i in range(count - 1) if holding[i] < limit]
        mass, budget = sum([portions[i] for i in free]), rest
        for i in free:
            more = min(limit - holding[i], max(1, budget * portions[i] // mass), rest)
            holding[i] = holding[i] + more
            rest = rest - more
    return np.array([limit] + holding)


def ragged(own_key, number_of, total, reach, lean):
    if number_of == 2:
        one = jax.random.randint(own_key, (), max(1, total - reach), min(reach, total - 1) + 1)
        return jnp.stack([one, total - one])
    lengths = jnp.asarray(split_up(number_of, total, reach, lean), jnp.int32)
    pairs = (number_of - 1) // 2
    donor, receiver = lengths[1:1 + 2 * pairs:2], lengths[2:2 + 2 * pairs:2]
    room = jnp.minimum(donor - 1, reach - receiver)
    passed = jax.random.randint(jax.random.fold_in(own_key, 1), (pairs,), 0, 1 << 20) % (room + 1)
    lengths = lengths.at[1:1 + 2 * pairs:2].set(donor - passed).at[2:2 + 2 * pairs:2].set(receiver + passed)
    return lengths[jax.random.permutation(jax.random.fold_in(own_key, 2), number_of)]


def gaussian(own_key, extent, spread, limit, cuts=(), kind=jnp.bfloat16):
    values = spread * jax.random.normal(own_key, extent, jnp.float32)
    if cuts:
        values = values * block_levels(own_key, extent, cuts, -0.22, 0.18)
    return jnp.clip(values, -limit, limit).astype(kind)


def setup_inputs(seed: int = 0) -> dict:
    streams_of = jax.random.split(jax.random.key(seed), 7)
    return {
        "queries": draw_queries(jax.random.fold_in(streams_of[6], 71), 0),
        "output_gradient": gaussian(streams_of[1], (WINDOW_TOKENS, QUERY_HEADS * HEAD_SIZE), 1.0, 6.0, ((0, 8), (1, 4))),
        "key_states": draw_key_states(jax.random.fold_in(streams_of[6], 71), 0),
        "value_inputs": gaussian(streams_of[3], (WINDOW_TOKENS, KEY_VALUE_HEADS * HEAD_SIZE), 1.0, 6.0, ((0, 32),)),
        "turn_ids": jnp.searchsorted(jnp.cumsum(ragged(streams_of[4], WINDOW_TOKENS // (4 * BLOCK_POSITIONS), WINDOW_TOKENS, BACK * BLOCK_POSITIONS, 2)), jnp.arange(WINDOW_TOKENS), side="right").astype(jnp.int32),
        "listed": with_ends((jax.random.randint(streams_of[5], (HEAD_GROUPS, NB, BACK), 0, 2) < 1).astype(jnp.int32), jax.random.fold_in(streams_of[5], 1), 0, 1),
    }


SCORE_SCALE = 1.0 / 12.0
NEG_LARGE = -1.0e30


def visible_mask(turn_ids, listed, query_begin, key_pos, tok_rows):
    query_pos = query_begin + jnp.arange(tok_rows, dtype=jnp.int32)
    query_turn = lax.dynamic_slice_in_dim(turn_ids, query_begin, tok_rows, 0)
    key_turn = turn_ids[jnp.clip(key_pos, 0, turn_ids.shape[0] - 1)]
    blk_count = tok_rows // BLOCK_POSITIONS
    query_blocks = query_begin // BLOCK_POSITIONS + jnp.arange(blk_count, dtype=jnp.int32)
    list_table = lax.dynamic_slice_in_dim(listed, query_begin // BLOCK_POSITIONS, blk_count, 1)
    offsets = query_blocks[:, None] - key_pos[None, :] // BLOCK_POSITIONS - 1
    onehot = (offsets[:, :, None] == jnp.arange(BACK, dtype=jnp.int32)[None, None, :]).astype(jnp.float32)
    listed_hit = jnp.einsum("gbo,bko->gbk", list_table.astype(jnp.float32), onehot) > 0.5
    listed_hit = jnp.repeat(listed_hit, BLOCK_POSITIONS, axis=1)
    causal_ok = (key_pos[None, :] <= query_pos[:, None]) & (key_pos[None, :] >= 0)
    same_turn = query_turn[:, None] == key_turn[None, :]
    return causal_ok[None] & (same_turn[None] | listed_hit)


def reference(queries, output_gradient, key_states, value_inputs, turn_ids, listed):
    group_width = QUERY_HEADS // KEY_VALUE_HEADS
    group_head_count = KEY_VALUE_HEADS // HEAD_GROUPS
    padding_rows = BACK * BLOCK_POSITIONS
    key_extent = (BACK + 1) * BLOCK_POSITIONS
    empty_rows = jnp.zeros((padding_rows, KEY_VALUE_HEADS * HEAD_SIZE), jnp.bfloat16)
    key_padded_rows = jnp.concatenate([empty_rows, key_states], axis=0)
    value_padded_rows = jnp.concatenate([empty_rows, value_inputs], axis=0)

    def per_block(running, blk_index):
        key_gradient, value_gradient = running
        query_begin = blk_index * BLOCK_POSITIONS
        query_block = lax.dynamic_slice_in_dim(queries, query_begin, BLOCK_POSITIONS, 0).astype(jnp.float32).reshape(BLOCK_POSITIONS, KEY_VALUE_HEADS, group_width, HEAD_SIZE)
        block_gradient = lax.dynamic_slice_in_dim(output_gradient, query_begin, BLOCK_POSITIONS, 0).astype(jnp.float32).reshape(BLOCK_POSITIONS, KEY_VALUE_HEADS, group_width, HEAD_SIZE)
        window_keys = lax.dynamic_slice_in_dim(key_padded_rows, query_begin, key_extent, 0).astype(jnp.float32).reshape(key_extent, KEY_VALUE_HEADS, HEAD_SIZE)
        window_values = lax.dynamic_slice_in_dim(value_padded_rows, query_begin, key_extent, 0).astype(jnp.float32).reshape(key_extent, KEY_VALUE_HEADS, HEAD_SIZE)
        key_pos = query_begin - padding_rows + jnp.arange(key_extent, dtype=jnp.int32)
        allowed = visible_mask(turn_ids, listed, query_begin, key_pos, BLOCK_POSITIONS)
        allowed_heads = jnp.repeat(allowed, group_head_count, axis=0)[:, None]
        raw_scores = jnp.einsum("rhqd,khd->hqrk", query_block, window_keys) * SCORE_SCALE
        scores = jnp.where(allowed_heads, raw_scores, NEG_LARGE)
        peak_max = jnp.max(scores, axis=3, keepdims=True)
        weights = jnp.where(allowed_heads, jnp.exp(scores - peak_max), 0.0)
        soft_prob = weights / jnp.sum(weights, axis=3, keepdims=True)
        grad_prob = jnp.einsum("rhqd,khd->hqrk", block_gradient, window_values)
        delta_row = jnp.sum(soft_prob * grad_prob, axis=3, keepdims=True)
        blended_rows = (SCORE_SCALE * soft_prob * (grad_prob - delta_row)).astype(jnp.bfloat16)
        blended_rows = lax.optimization_barrier(blended_rows).astype(jnp.float32)
        probability_floor = lax.optimization_barrier(soft_prob.astype(jnp.bfloat16)).astype(jnp.float32)
        grad_q_blk = jnp.einsum("hqrk,khd->rhqd", blended_rows, window_keys).reshape(BLOCK_POSITIONS, QUERY_HEADS * HEAD_SIZE)
        window_key_gradient = jnp.einsum("tmev,etmi->vti", blended_rows, query_block).reshape(key_extent, KEY_VALUE_HEADS * HEAD_SIZE)
        window_value_gradient = jnp.einsum("tmev,etmi->vti", probability_floor, block_gradient).reshape(key_extent, KEY_VALUE_HEADS * HEAD_SIZE)
        key_gradient = lax.dynamic_update_slice_in_dim(key_gradient, lax.dynamic_slice_in_dim(key_gradient, query_begin, key_extent, 0) + window_key_gradient, query_begin, 0)
        value_gradient = lax.dynamic_update_slice_in_dim(value_gradient, lax.dynamic_slice_in_dim(value_gradient, query_begin, key_extent, 0) + window_value_gradient, query_begin, 0)
        return (key_gradient, value_gradient), grad_q_blk

    initial_state = (jnp.zeros((WINDOW_TOKENS + padding_rows, KEY_VALUE_HEADS * HEAD_SIZE), jnp.float32), jnp.zeros((WINDOW_TOKENS + padding_rows, KEY_VALUE_HEADS * HEAD_SIZE), jnp.float32))
    (key_gradient, value_gradient), grad_q_blocks = lax.scan(per_block, initial_state, jnp.arange(NB, dtype=jnp.int32))
    return grad_q_blocks.reshape(WINDOW_TOKENS, QUERY_HEADS * HEAD_SIZE), key_gradient[padding_rows:], value_gradient[padding_rows:]
```

```python
import functools

import jax
import jax.numpy as jnp
from jax import lax
from jax.experimental import pallas as pl
from jax.experimental.pallas import tpu as pltpu
from jax.sharding import PartitionSpec as P

QUERY_HEADS = 32
KEY_VALUE_HEADS = 16
HEAD_SIZE = 128
HEAD_GROUPS = 2
BLOCK_POSITIONS = 128
BACK = 14

SCORE_SCALE = 1.0 / 12.0
LOG2E = 1.4426950408889634
NEG_LARGE = -1e30
HIT = 1 << 20
NO_KEY = -(1 << 24)
TILE = 256
MESH = pl.DeviceIdType.MESH
VMEM_LIMIT = 48 * 1024 * 1024


class Place:
    def __init__(self, spans, ka_count):
        self.spans = spans
        self.ka_count = ka_count
        pb = lax.axis_index("pb")
        self.ka = lax.axis_index("ka")
        self.group = pb // spans
        self.span = pb % spans
        self.pair = self.ka // 2
        self.core = self.ka % 2
        self.head = self.pair * spans + self.span
        self.held = KEY_VALUE_HEADS // ka_count

    def at(self, span, ka):
        return {"pb": self.group * self.spans + span, "ka": ka}

    def greet(self):
        barrier = pltpu.get_barrier_semaphore()
        for t in range(1, self.spans * self.ka_count):
            pl.semaphore_signal(
                barrier,
                inc=1,
                device_id=self.at(
                    (self.span + t // self.ka_count) % self.spans,
                    (self.ka + t % self.ka_count) % self.ka_count,
                ),
                device_id_type=MESH,
            )
        pl.semaphore_wait(barrier, self.spans * self.ka_count - 1)


def wait_for(ref, sem):
    pltpu.make_async_copy(ref, ref, sem).wait()


def lanes(index):
    return pl.ds(pl.multiple_of(index * HEAD_SIZE, HEAD_SIZE), HEAD_SIZE)


def rows_at(begin, count):
    return pl.ds(pl.multiple_of(begin, count), count)


def gather_kernel(
    spans, ka_count, q, do, k, v, qh, doh, kh, vh, kv_send, kv_recv, q_send, q_recv, x_send, x_recv
):
    me = Place(spans, ka_count)
    tok = q.shape[0]
    piece = k.shape[0]
    me.greet()
    kv_rows = rows_at(me.span * tok + me.ka * piece, piece)
    for t in range(spans * ka_count // 2):
        span = (me.span + t % spans) % spans
        pair = (me.pair + t // spans) % (ka_count // 2)
        cols = lanes(pair * spans + span)
        for core, (src, dst) in enumerate(((k, kh), (v, vh))):

            def remote(src=src, dst=dst, core=core, span=span, pair=pair, cols=cols):
                pltpu.make_async_remote_copy(
                    src_ref=src.at[:, cols],
                    dst_ref=dst.at[kv_rows, :],
                    send_sem=kv_send,
                    recv_sem=kv_recv,
                    device_id=me.at(span, 2 * pair + core),
                    device_id_type=MESH,
                ).start()

            if t == 0:
                pl.when(me.core != core)(remote)

                @pl.when(me.core == core)
                def _(src=src, dst=dst, cols=cols):
                    pltpu.make_async_copy(src.at[:, cols], dst.at[kv_rows, :], kv_recv).start()
            else:
                remote()
    q_rows = rows_at(me.span * tok, tok)
    for j in range(me.held):
        near = (me.span + j) % me.held
        span = me.held * me.core + near
        for core in range(2):
            cols = lanes(2 * near + core)
            mine = (span == me.span) & (me.core == core)
            for which, (src, dst) in enumerate(((q, qh), (do, doh))):

                @pl.when(mine)
                def _(src=src, dst=dst, cols=cols, which=which):
                    pltpu.make_async_copy(
                        src.at[:, cols], dst.at[q_rows, :], q_recv.at[which]
                    ).start()

                @pl.when(jnp.logical_not(mine))
                def _(src=src, dst=dst, cols=cols, core=core, span=span, which=which):
                    pltpu.make_async_remote_copy(
                        src_ref=src.at[:, cols],
                        dst_ref=dst.at[q_rows, :],
                        send_sem=q_send.at[which],
                        recv_sem=q_recv.at[which],
                        device_id=me.at(span, 2 * me.pair + core),
                        device_id_type=MESH,
                    ).start()

    def exchange(ref):
        return pltpu.make_async_remote_copy(
            src_ref=ref,
            dst_ref=ref,
            send_sem=x_send,
            recv_sem=x_recv,
            device_id=me.at(me.span, 2 * me.pair + 1 - me.core),
            device_id_type=MESH,
        )

    for core, ref in enumerate((kh, vh)):

        @pl.when(me.core == core)
        def _(ref=ref):
            wait_for(ref, kv_recv)
            exchange(ref).start()

    wait_for(kh, x_recv)
    wait_for(kh, x_send)
    wait_for(kh.at[: (spans * ka_count - 1) * piece], kv_send)
    wait_for(qh, q_recv.at[0])
    wait_for(doh, q_recv.at[1])
    sent = 2 * me.held * tok
    has_own = me.span // me.held == me.core
    for which, ref in enumerate((qh, doh)):
        sem = q_send.at[which]
        pl.when(has_own)(lambda ref=ref, sem=sem: wait_for(ref.at[: sent - tok], sem))
        pl.when(jnp.logical_not(has_own))(lambda ref=ref, sem=sem: wait_for(ref.at[:sent], sem))


def attention_kernel(
    spans, ka_count, halo, listed, turn_row, turn_col, q, do, k, v, dq, dk, dv, kt, s_buf, g_buf
):
    me = Place(spans, ka_count)
    rows = q.shape[0]
    keys = k.shape[0]
    blocks = listed.shape[0] // (HEAD_GROUPS * BACK)
    head_group = me.head // (KEY_VALUE_HEADS // HEAD_GROUPS)
    list_base = (head_group * blocks + me.group * (rows // BLOCK_POSITIONS)) * BACK
    dk[...] = jnp.zeros_like(dk)
    dv[...] = jnp.zeros_like(dv)
    for n in range(keys // TILE):
        kt[:, n * TILE : (n + 1) * TILE] = k[n * TILE : (n + 1) * TILE, :].T
    left = lax.broadcasted_iota(jnp.int32, (1, TILE), 1) < BLOCK_POSITIONS
    causal = lax.broadcasted_iota(jnp.int32, (TILE, TILE), 0) <= lax.broadcasted_iota(
        jnp.int32, (TILE, TILE), 1
    )

    def hit(block, key_block):
        offset = block - key_block - 1
        if 0 <= offset < BACK:
            return listed[list_base + block * BACK + offset]
        return jnp.int32(0)

    for i in reversed(range(rows // TILE)):
        q_i = q[i * TILE : (i + 1) * TILE, :]
        do_i = do[i * TILE : (i + 1) * TILE, :]
        turn_i = turn_row[:, i * TILE : (i + 1) * TILE]
        last = halo // TILE + i
        first = max(0, last - BACK * BLOCK_POSITIONS // TILE)
        peak = jnp.full((8, TILE), NEG_LARGE, jnp.float32)
        for n in range(first, last + 1):
            at = slice(n * TILE, (n + 1) * TILE)
            s = lax.dot_general(
                k[at, :], q_i, (((1,), (1,)), ((), ())), preferred_element_type=jnp.float32
            ) * (SCORE_SCALE * LOG2E)
            parts = []
            for half in range(TILE // BLOCK_POSITIONS):
                key_block = 2 * n + half - halo // BLOCK_POSITIONS
                seen = jnp.where(left, hit(2 * i, key_block), hit(2 * i + 1, key_block))
                bar = turn_i - seen * HIT
                begin = n * TILE + half * BLOCK_POSITIONS
                turns = turn_col[begin : begin + BLOCK_POSITIONS, :]
                parts.append(jnp.concatenate([turns, turns], axis=1) >= bar)
            allowed = jnp.concatenate(parts, axis=0)
            if n == last:
                allowed = allowed & causal
            s = jnp.where(allowed, s, NEG_LARGE)
            s_buf[at, :] = s
            peak = jnp.maximum(peak, jnp.max(s.reshape(TILE // 8, 8, TILE), axis=0))
        peak = jnp.max(peak, axis=0, keepdims=True)
        total = jnp.zeros((8, TILE), jnp.float32)
        inner = jnp.zeros((8, TILE), jnp.float32)
        for n in range(first, last + 1):
            at = slice(n * TILE, (n + 1) * TILE)
            g = lax.dot_general(
                v[at, :], do_i, (((1,), (1,)), ((), ())), preferred_element_type=jnp.float32
            )
            p = jnp.exp2(s_buf[at, :] - peak)
            s_buf[at, :] = p
            g_buf[at, :] = g
            total = total + jnp.sum(p.reshape(TILE // 8, 8, TILE), axis=0)
            inner = inner + jnp.sum((p * g).reshape(TILE // 8, 8, TILE), axis=0)
        inverse = 1.0 / jnp.sum(total, axis=0, keepdims=True)
        delta = jnp.sum(inner, axis=0, keepdims=True) * inverse
        scaled = inverse * SCORE_SCALE
        dq_t = jnp.zeros((HEAD_SIZE, TILE), jnp.float32)
        for n in range(first, last + 1):
            at = slice(n * TILE, (n + 1) * TILE)
            p = s_buf[at, :]
            mixed = ((p * scaled) * (g_buf[at, :] - delta)).astype(jnp.bfloat16)
            low = (p * inverse).astype(jnp.bfloat16)
            dv[at, :] += jnp.dot(low, do_i, preferred_element_type=jnp.float32)
            dk[at, :] += jnp.dot(mixed, q_i, preferred_element_type=jnp.float32)
            dq_t = dq_t + jnp.dot(kt[:, at], mixed, preferred_element_type=jnp.float32)
        dq[i * TILE : (i + 1) * TILE, :] = dq_t.T.astype(jnp.bfloat16)


def scatter_kernel(
    spans, ka_count, dqh, dkh, dvh, dq, dk, dv, got, low, x_send, x_recv, q_send, q_recv, kv_send, kv_recv
):
    me = Place(spans, ka_count)
    tok = dq.shape[0]
    piece = dk.shape[0]
    me.greet()

    def exchange(ref):
        return pltpu.make_async_remote_copy(
            src_ref=ref,
            dst_ref=got,
            send_sem=x_send,
            recv_sem=x_recv,
            device_id=me.at(me.span, 2 * me.pair + 1 - me.core),
            device_id_type=MESH,
        )

    pl.when(me.core == 0)(lambda: exchange(dvh).start())
    pl.when(me.core == 1)(lambda: exchange(dkh).start())
    owner = 2 * me.pair + me.span // me.held
    cols = lanes(2 * (me.span % me.held) + me.core)
    for t in range(spans):
        span = (me.span + t) % spans
        src = dqh.at[rows_at(span * tok, tok), :]

        def remote(src=src, span=span):
            pltpu.make_async_remote_copy(
                src_ref=src,
                dst_ref=dq.at[:, cols],
                send_sem=q_send,
                recv_sem=q_recv,
                device_id=me.at(span, owner),
                device_id_type=MESH,
            ).start()

        if t == 0:
            pl.when(owner != me.ka)(remote)

            @pl.when(owner == me.ka)
            def _(src=src):
                pltpu.make_async_copy(src, dq.at[:, cols], q_recv).start()
        else:
            remote()
    wait_for(got, x_recv)
    for core, (own, out) in enumerate(((dkh, dk), (dvh, dv))):

        @pl.when(me.core == core)
        def _(own=own, out=out):
            low[...] = (own[...] + got[...]).astype(jnp.bfloat16)
            head_cols = lanes(me.head)
            for t in range(spans * ka_count):
                span = (me.span + t // ka_count) % spans
                ka = (me.ka + t % ka_count) % ka_count
                src = low.at[rows_at(span * tok + ka * piece, piece), :]
                dst = out.at[:, head_cols]
                if t == 0:
                    pltpu.make_async_copy(src, dst, kv_recv.at[core]).start()
                else:
                    pltpu.make_async_remote_copy(
                        src_ref=src,
                        dst_ref=dst,
                        send_sem=kv_send,
                        recv_sem=kv_recv.at[core],
                        device_id=me.at(span, ka),
                        device_id_type=MESH,
                    ).start()

    wait_for(got, x_send)
    sent = spans * tok
    pl.when(owner == me.ka)(lambda: wait_for(dqh.at[: sent - tok], q_send))
    pl.when(owner != me.ka)(lambda: wait_for(dqh.at[:sent], q_send))
    wait_for(dq, q_recv)
    wait_for(low.at[: (spans * ka_count - 1) * piece], kv_send)
    wait_for(dk, kv_recv.at[0])
    wait_for(dv, kv_recv.at[1])


def per_device(queries, output_gradient, key_states, value_inputs, turn_ids, listed):
    ka_count = lax.axis_size("ka")
    pb_count = lax.axis_size("pb")
    spans = 2 * KEY_VALUE_HEADS // ka_count
    groups = pb_count // spans
    tok = queries.shape[0]
    piece = key_states.shape[0]
    rows = spans * tok
    halo = rows if groups > 1 else 0
    bf16, f32 = jnp.bfloat16, jnp.float32
    any_space = pl.BlockSpec(memory_space=pl.ANY)
    vmem = pl.BlockSpec(memory_space=pltpu.VMEM)
    dma = pltpu.SemaphoreType.DMA
    head_rows = jax.ShapeDtypeStruct((rows, HEAD_SIZE), bf16)

    q, do, k, v = pl.pallas_call(
        functools.partial(gather_kernel, spans, ka_count),
        out_shape=[head_rows] * 4,
        in_specs=[any_space] * 4,
        out_specs=[any_space] * 4,
        scratch_shapes=[dma, dma, dma((2,)), dma((2,)), dma, dma],
        compiler_params=pltpu.CompilerParams(collective_id=0, has_side_effects=True),
        name="gather_heads",
    )(queries, output_gradient, key_states, value_inputs)

    group = lax.axis_index("pb") // spans
    if groups > 1:
        turn_own = lax.dynamic_slice_in_dim(turn_ids, group * rows, rows, 0)
        turn_before = lax.dynamic_slice_in_dim(
            turn_ids, jnp.maximum(group - 1, 0) * rows, rows, 0
        )
        turn_before = jnp.where(group > 0, turn_before, NO_KEY)
        turn_keys = jnp.concatenate([turn_before, turn_own])
        forward = [(i, i + spans) for i in range(pb_count - spans)]
        k_before, v_before = lax.ppermute(jnp.stack([k, v]), "pb", forward)
        k = jnp.concatenate([k_before, k])
        v = jnp.concatenate([v_before, v])
    else:
        turn_own = turn_keys = turn_ids
    keys = halo + rows
    key_grad = jax.ShapeDtypeStruct((keys, HEAD_SIZE), f32)
    dq, dk, dv = pl.pallas_call(
        functools.partial(attention_kernel, spans, ka_count, halo),
        out_shape=[head_rows, key_grad, key_grad],
        in_specs=[pl.BlockSpec(memory_space=pltpu.SMEM)] + [vmem] * 6,
        out_specs=[vmem] * 3,
        scratch_shapes=[
            pltpu.VMEM((HEAD_SIZE, keys), bf16),
            pltpu.VMEM((keys, TILE), f32),
            pltpu.VMEM((keys, TILE), f32),
        ],
        compiler_params=pltpu.CompilerParams(vmem_limit_bytes=VMEM_LIMIT),
        name="attention_backward",
    )(
        listed.reshape(-1),
        turn_own[None, :],
        jnp.broadcast_to(turn_keys[:, None], (keys, HEAD_SIZE)),
        q,
        do,
        k,
        v,
    )
    if groups > 1:
        back = [(i + spans, i) for i in range(pb_count - spans)]
        dk_later, dv_later = lax.ppermute(jnp.stack([dk[:halo], dv[:halo]]), "pb", back)
        dk = dk[halo:] + dk_later
        dv = dv[halo:] + dv_later

    out = pl.pallas_call(
        functools.partial(scatter_kernel, spans, ka_count),
        out_shape=[
            jax.ShapeDtypeStruct(queries.shape, bf16),
            jax.ShapeDtypeStruct(key_states.shape, bf16),
            jax.ShapeDtypeStruct(key_states.shape, bf16),
        ],
        in_specs=[vmem] * 3,
        out_specs=[any_space] * 3,
        scratch_shapes=[
            pltpu.VMEM((rows, HEAD_SIZE), f32),
            pltpu.VMEM((rows, HEAD_SIZE), bf16),
            dma,
            dma,
            dma,
            dma,
            dma,
            dma((2,)),
        ],
        compiler_params=pltpu.CompilerParams(
            collective_id=1, has_side_effects=True, vmem_limit_bytes=VMEM_LIMIT
        ),
        name="scatter_gradients",
    )(dq, dk, dv)
    return tuple(part.astype(f32) for part in out)


def solution(mesh):
    in_specs = (
        P("pb", "ka"),
        P("pb", "ka"),
        P(("pb", "ka"), None),
        P(("pb", "ka"), None),
        P(),
        P(),
    )
    out_specs = (P("pb", "ka"), P(("pb", "ka"), None), P(("pb", "ka"), None))
    return jax.shard_map(
        per_device, mesh=mesh, in_specs=in_specs, out_specs=out_specs, check_vma=False
    )
```

```python
import functools

import jax
import jax.numpy as jnp
from jax import lax
from jax.experimental import pallas as pl
from jax.experimental.pallas import tpu as pltpu
from jax.sharding import PartitionSpec as P

QUERY_HEADS = 32
KEY_VALUE_HEADS = 16
HEAD_SIZE = 128
HEAD_GROUPS = 2
BLOCK_POSITIONS = 128
BACK = 14

SCORE_SCALE = 1.0 / 12.0
LOG2E = 1.4426950408889634
NEG_LARGE = -1e30
HIT = float(1 << 20)
NO_KEY = -(1 << 22)
TILE = 256
MESH = pl.DeviceIdType.MESH
VMEM_LIMIT = 48 * 1024 * 1024


class Place:
    def __init__(self, spans, ka_count):
        self.spans = spans
        self.ka_count = ka_count
        pb = lax.axis_index("pb")
        self.ka = lax.axis_index("ka")
        self.group = pb // spans
        self.span = pb % spans
        self.pair = self.ka // 2
        self.core = self.ka % 2
        self.head = self.pair * spans + self.span
        self.held = KEY_VALUE_HEADS // ka_count

    def at(self, span, ka):
        return {"pb": self.group * self.spans + span, "ka": ka}

    def greet(self):
        barrier = pltpu.get_barrier_semaphore()
        for t in range(1, self.spans * self.ka_count):
            pl.semaphore_signal(
                barrier,
                inc=1,
                device_id=self.at(
                    (self.span + t // self.ka_count) % self.spans,
                    (self.ka + t % self.ka_count) % self.ka_count,
                ),
                device_id_type=MESH,
            )
        pl.semaphore_wait(barrier, self.spans * self.ka_count - 1)


def wait_for(ref, sem):
    pltpu.make_async_copy(ref, ref, sem).wait()


def lanes(index):
    return pl.ds(pl.multiple_of(index * HEAD_SIZE, HEAD_SIZE), HEAD_SIZE)


def rows_at(begin, count):
    return pl.ds(pl.multiple_of(begin, count), count)


def send_heads(me, q, do, k, v, qh, doh, kh, vh, kv_send, kv_recv, q_send, q_recv):
    tok = q.shape[0]
    piece = k.shape[0]
    kv_rows = rows_at(me.span * tok + me.ka * piece, piece)
    for t in range(me.spans * me.ka_count // 2):
        span = (me.span + t % me.spans) % me.spans
        pair = (me.pair + t // me.spans) % (me.ka_count // 2)
        cols = lanes(pair * me.spans + span)
        for core, (src, dst) in enumerate(((k, kh), (v, vh))):

            def remote(src=src, dst=dst, core=core, span=span, pair=pair, cols=cols):
                pltpu.make_async_remote_copy(
                    src_ref=src.at[:, cols],
                    dst_ref=dst.at[kv_rows, :],
                    send_sem=kv_send,
                    recv_sem=kv_recv,
                    device_id=me.at(span, 2 * pair + core),
                    device_id_type=MESH,
                ).start()

            if t == 0:
                pl.when(me.core != core)(remote)

                @pl.when(me.core == core)
                def _(src=src, dst=dst, cols=cols):
                    pltpu.make_async_copy(src.at[:, cols], dst.at[kv_rows, :], kv_recv).start()
            else:
                remote()
    q_rows = rows_at(me.span * tok, tok)
    for j in range(me.held):
        near = (me.span + j) % me.held
        span = me.held * me.core + near
        for core in range(2):
            cols = lanes(2 * near + core)
            mine = (span == me.span) & (me.core == core)
            for which, (src, dst) in enumerate(((q, qh), (do, doh))):
                sem = q_recv.at[which, me.span]

                @pl.when(mine)
                def _(src=src, dst=dst, cols=cols, sem=sem):
                    pltpu.make_async_copy(src.at[:, cols], dst.at[q_rows, :], sem).start()

                @pl.when(jnp.logical_not(mine))
                def _(src=src, dst=dst, cols=cols, core=core, span=span, which=which, sem=sem):
                    pltpu.make_async_remote_copy(
                        src_ref=src.at[:, cols],
                        dst_ref=dst.at[q_rows, :],
                        send_sem=q_send.at[which],
                        recv_sem=sem,
                        device_id=me.at(span, 2 * me.pair + core),
                        device_id_type=MESH,
                    ).start()


def to_other_core(me, src, dst, send_sem, recv_sem):
    return pltpu.make_async_remote_copy(
        src_ref=src,
        dst_ref=dst,
        send_sem=send_sem,
        recv_sem=recv_sem,
        device_id=me.at(me.span, 2 * me.pair + 1 - me.core),
        device_id_type=MESH,
    )


def share_keys(me, kh, vh, kv_recv, x_send, x_recv):
    for core, ref in enumerate((kh, vh)):

        @pl.when(me.core == core)
        def _(ref=ref):
            wait_for(ref, kv_recv)
            to_other_core(me, ref, ref, x_send, x_recv).start()

    wait_for(kh, x_recv)


def finish_heads(me, qh, doh, kh, kv_send, q_send, x_send, tok, piece):
    wait_for(kh, x_send)
    wait_for(kh.at[: (me.spans * me.ka_count - 1) * piece], kv_send)
    sent = 2 * me.held * tok
    has_own = me.span // me.held == me.core
    for which, ref in enumerate((qh, doh)):
        sem = q_send.at[which]
        pl.when(has_own)(lambda ref=ref, sem=sem: wait_for(ref.at[: sent - tok], sem))
        pl.when(jnp.logical_not(has_own))(lambda ref=ref, sem=sem: wait_for(ref.at[:sent], sem))


def gather_kernel(
    spans, ka_count, q, do, k, v, qh, doh, kh, vh, kv_send, kv_recv, q_send, q_recv, x_send, x_recv
):
    me = Place(spans, ka_count)
    tok = q.shape[0]
    me.greet()
    send_heads(me, q, do, k, v, qh, doh, kh, vh, kv_send, kv_recv, q_send, q_recv)
    share_keys(me, kh, vh, kv_recv, x_send, x_recv)
    for span in range(spans):
        wait_for(qh.at[span * tok : (span + 1) * tok], q_recv.at[0, span])
        wait_for(doh.at[span * tok : (span + 1) * tok], q_recv.at[1, span])
    finish_heads(me, qh, doh, kh, kv_send, q_send, x_send, tok, k.shape[0])


def fused_kernel(
    spans, ka_count, listed, turn_row, q, do, k, v, dq, dk, dv,
    qh, doh, kh, vh, turn_col, kt, s_buf, g_buf, dqh, dkh, dvh, got, low,
    kv_send, kv_recv, q_send, q_recv, k_send, k_recv,
    x_send, x_recv, dq_send, dq_recv, dkv_send, dkv_recv,
):
    me = Place(spans, ka_count)
    tok = q.shape[0]
    piece = k.shape[0]
    me.greet()
    send_heads(me, q, do, k, v, qh, doh, kh, vh, kv_send, kv_recv, q_send, q_recv)
    for n in range(turn_col.shape[0] // HEAD_SIZE):
        at = slice(n * HEAD_SIZE, (n + 1) * HEAD_SIZE)
        turn_col[at, :] = jnp.broadcast_to(turn_row[:, at], (HEAD_SIZE, HEAD_SIZE)).T
    share_keys(me, kh, vh, kv_recv, k_send, k_recv)
    owner = 2 * me.pair + me.span // me.held
    q_cols = lanes(2 * (me.span % me.held) + me.core)
    head_cols = lanes(me.head)

    def ready(i):
        wait_for(qh.at[i * tok : (i + 1) * tok], q_recv.at[0, i])
        wait_for(doh.at[i * tok : (i + 1) * tok], q_recv.at[1, i])

    def send_queries(i):
        src = dqh.at[i * tok : (i + 1) * tok, :]
        mine = (me.span == i) & (owner == me.ka)

        @pl.when(mine)
        def _():
            pltpu.make_async_copy(src, dq.at[:, q_cols], dq_recv).start()

        @pl.when(jnp.logical_not(mine))
        def _():
            pltpu.make_async_remote_copy(
                src_ref=src,
                dst_ref=dq.at[:, q_cols],
                send_sem=dq_send,
                recv_sem=dq_recv,
                device_id=me.at(i, owner),
                device_id_type=MESH,
            ).start()

    def share_grads(j):
        at = slice(j * tok, (j + 1) * tok)
        for core, ref in enumerate((dvh, dkh)):

            @pl.when(me.core == core)
            def _(ref=ref):
                to_other_core(me, ref.at[at], got.at[at], x_send, x_recv.at[j]).start()

    def send_grads(j):
        at = slice(j * tok, (j + 1) * tok)
        wait_for(got.at[at], x_recv.at[j])
        for core, (own, out) in enumerate(((dkh, dk), (dvh, dv))):

            @pl.when(me.core == core)
            def _(own=own, out=out, core=core):
                low[at, :] = (own[at, :] + got[at, :]).astype(jnp.bfloat16)
                for t in range(ka_count):
                    ka = (me.ka + t) % ka_count
                    src = low.at[rows_at(j * tok + ka * piece, piece), :]
                    dst = out.at[:, head_cols]

                    def remote(src=src, dst=dst, ka=ka):
                        pltpu.make_async_remote_copy(
                            src_ref=src,
                            dst_ref=dst,
                            send_sem=dkv_send,
                            recv_sem=dkv_recv.at[core],
                            device_id=me.at(j, ka),
                            device_id_type=MESH,
                        ).start()

                    if t == 0:
                        pl.when(me.span != j)(remote)

                        @pl.when(me.span == j)
                        def _(src=src, dst=dst):
                            pltpu.make_async_copy(src, dst, dkv_recv.at[core]).start()
                    else:
                        remote()

    half = spans // 2
    order = [spans - 1, *range(half), *range(spans - 2, half - 1, -1)]
    done = set()
    shared = []

    def after(i):
        send_queries(i)
        done.add(i)
        for j in shared:
            send_grads(j)
        shared.clear()
        for j in range(spans - 1, -1, -1):
            if j not in started and all(n in done for n in range(j, spans)):
                share_grads(j)
                started.add(j)
                shared.append(j)

    started = set()
    attend(
        me, 0, order, ready, after,
        listed, turn_row, turn_col, qh, doh, kh, vh, dqh, dkh, dvh, kt, s_buf, g_buf,
    )
    for j in shared:
        send_grads(j)
    finish_heads(me, qh, doh, kh, kv_send, q_send, k_send, tok, piece)
    wait_for(got, x_send)
    sent = spans * tok
    pl.when(owner == me.ka)(lambda: wait_for(dqh.at[: sent - tok], dq_send))
    pl.when(owner != me.ka)(lambda: wait_for(dqh.at[:sent], dq_send))
    wait_for(low.at[: (spans * ka_count - 1) * piece], dkv_send)
    wait_for(dq, dq_recv)
    wait_for(dk, dkv_recv.at[0])
    wait_for(dv, dkv_recv.at[1])


def attention_kernel(spans, ka_count, halo, *refs):
    order = list(range(refs[3].shape[0] // TILE))
    nothing = lambda i: None
    attend(Place(spans, ka_count), halo, order, nothing, nothing, *refs)


def attend(
    me, halo, order, ready, after,
    listed, turn_row, turn_col, q, do, k, v, dq, dk, dv, kt, s_buf, g_buf,
):
    rows = q.shape[0]
    keys = k.shape[0]
    blocks = listed.shape[0] // (HEAD_GROUPS * BACK)
    head_group = me.head // (KEY_VALUE_HEADS // HEAD_GROUPS)
    list_base = (head_group * blocks + me.group * (rows // BLOCK_POSITIONS)) * BACK
    dk[...] = jnp.zeros_like(dk)
    dv[...] = jnp.zeros_like(dv)
    for n in range(keys // TILE):
        kt[:, n * TILE : (n + 1) * TILE] = k[n * TILE : (n + 1) * TILE, :].T
    left = lax.broadcasted_iota(jnp.int32, (1, TILE), 1) < BLOCK_POSITIONS
    causal = lax.broadcasted_iota(jnp.int32, (TILE, TILE), 0) <= lax.broadcasted_iota(
        jnp.int32, (TILE, TILE), 1
    )

    def hit(block, key_block):
        offset = block - key_block - 1
        if 0 <= offset < BACK:
            return listed[list_base + block * BACK + offset]
        return jnp.int32(0)

    for i in order:
        ready(i)
        q_i = q[i * TILE : (i + 1) * TILE, :]
        do_i = do[i * TILE : (i + 1) * TILE, :]
        turn_i = turn_row[:, i * TILE : (i + 1) * TILE]
        last = halo // TILE + i
        first = max(0, last - BACK * BLOCK_POSITIONS // TILE)
        peak = jnp.full((8, TILE), NEG_LARGE, jnp.float32)
        for n in range(first, last + 1):
            at = slice(n * TILE, (n + 1) * TILE)
            s = lax.dot_general(
                k[at, :], q_i, (((1,), (1,)), ((), ())), preferred_element_type=jnp.float32
            ) * (SCORE_SCALE * LOG2E)
            parts = []
            for half in range(TILE // BLOCK_POSITIONS):
                key_block = 2 * n + half - halo // BLOCK_POSITIONS
                seen = jnp.where(left, hit(2 * i, key_block), hit(2 * i + 1, key_block))
                bar = turn_i - seen.astype(jnp.float32) * HIT
                begin = n * TILE + half * BLOCK_POSITIONS
                turns = turn_col[begin : begin + BLOCK_POSITIONS, :]
                parts.append(jnp.concatenate([turns, turns], axis=1) >= bar)
            allowed = jnp.concatenate(parts, axis=0)
            if n == last:
                allowed = allowed & causal
            s = jnp.where(allowed, s, NEG_LARGE)
            s_buf[at, :] = s
            peak = jnp.maximum(peak, jnp.max(s.reshape(TILE // 8, 8, TILE), axis=0))
        peak = jnp.max(peak, axis=0, keepdims=True)
        total = jnp.zeros((8, TILE), jnp.float32)
        inner = jnp.zeros((8, TILE), jnp.float32)
        for n in range(first, last + 1):
            at = slice(n * TILE, (n + 1) * TILE)
            g = lax.dot_general(
                v[at, :], do_i, (((1,), (1,)), ((), ())), preferred_element_type=jnp.float32
            )
            p = jnp.exp2(s_buf[at, :] - peak)
            s_buf[at, :] = p
            g_buf[at, :] = g
            total = total + jnp.sum(p.reshape(TILE // 8, 8, TILE), axis=0)
            inner = inner + jnp.sum((p * g).reshape(TILE // 8, 8, TILE), axis=0)
        inverse = 1.0 / jnp.sum(total, axis=0, keepdims=True)
        delta = jnp.sum(inner, axis=0, keepdims=True) * inverse
        scaled = inverse * SCORE_SCALE
        dq_t = jnp.zeros((HEAD_SIZE, TILE), jnp.float32)
        for n in range(first, last + 1):
            at = slice(n * TILE, (n + 1) * TILE)
            p = s_buf[at, :]
            mixed = ((p * scaled) * (g_buf[at, :] - delta)).astype(jnp.bfloat16)
            low = (p * inverse).astype(jnp.bfloat16)
            dv[at, :] += jnp.dot(low, do_i, preferred_element_type=jnp.float32)
            dk[at, :] += jnp.dot(mixed, q_i, preferred_element_type=jnp.float32)
            dq_t = dq_t + jnp.dot(kt[:, at], mixed, preferred_element_type=jnp.float32)
        dq[i * TILE : (i + 1) * TILE, :] = dq_t.T.astype(jnp.bfloat16)
        after(i)


def scatter_kernel(
    spans, ka_count, dqh, dkh, dvh, dq, dk, dv, got, low, x_send, x_recv, q_send, q_recv, kv_send, kv_recv
):
    me = Place(spans, ka_count)
    tok = dq.shape[0]
    piece = dk.shape[0]
    me.greet()

    def exchange(ref):
        return pltpu.make_async_remote_copy(
            src_ref=ref,
            dst_ref=got,
            send_sem=x_send,
            recv_sem=x_recv,
            device_id=me.at(me.span, 2 * me.pair + 1 - me.core),
            device_id_type=MESH,
        )

    pl.when(me.core == 0)(lambda: exchange(dvh).start())
    pl.when(me.core == 1)(lambda: exchange(dkh).start())
    owner = 2 * me.pair + me.span // me.held
    cols = lanes(2 * (me.span % me.held) + me.core)
    for t in range(spans):
        span = (me.span + t) % spans
        src = dqh.at[rows_at(span * tok, tok), :]

        def remote(src=src, span=span):
            pltpu.make_async_remote_copy(
                src_ref=src,
                dst_ref=dq.at[:, cols],
                send_sem=q_send,
                recv_sem=q_recv,
                device_id=me.at(span, owner),
                device_id_type=MESH,
            ).start()

        if t == 0:
            pl.when(owner != me.ka)(remote)

            @pl.when(owner == me.ka)
            def _(src=src):
                pltpu.make_async_copy(src, dq.at[:, cols], q_recv).start()
        else:
            remote()
    wait_for(got, x_recv)
    for core, (own, out) in enumerate(((dkh, dk), (dvh, dv))):

        @pl.when(me.core == core)
        def _(own=own, out=out):
            low[...] = (own[...] + got[...]).astype(jnp.bfloat16)
            head_cols = lanes(me.head)
            for t in range(spans * ka_count):
                span = (me.span + t // ka_count) % spans
                ka = (me.ka + t % ka_count) % ka_count
                src = low.at[rows_at(span * tok + ka * piece, piece), :]
                dst = out.at[:, head_cols]
                if t == 0:
                    pltpu.make_async_copy(src, dst, kv_recv.at[core]).start()
                else:
                    pltpu.make_async_remote_copy(
                        src_ref=src,
                        dst_ref=dst,
                        send_sem=kv_send,
                        recv_sem=kv_recv.at[core],
                        device_id=me.at(span, ka),
                        device_id_type=MESH,
                    ).start()

    wait_for(got, x_send)
    sent = spans * tok
    pl.when(owner == me.ka)(lambda: wait_for(dqh.at[: sent - tok], q_send))
    pl.when(owner != me.ka)(lambda: wait_for(dqh.at[:sent], q_send))
    wait_for(dq, q_recv)
    wait_for(low.at[: (spans * ka_count - 1) * piece], kv_send)
    wait_for(dk, kv_recv.at[0])
    wait_for(dv, kv_recv.at[1])


def per_device(queries, output_gradient, key_states, value_inputs, turn_ids, listed):
    ka_count = lax.axis_size("ka")
    pb_count = lax.axis_size("pb")
    spans = 2 * KEY_VALUE_HEADS // ka_count
    groups = pb_count // spans
    tok = queries.shape[0]
    piece = key_states.shape[0]
    rows = spans * tok
    halo = rows
    bf16, f32 = jnp.bfloat16, jnp.float32
    any_space = pl.BlockSpec(memory_space=pl.ANY)
    vmem = pl.BlockSpec(memory_space=pltpu.VMEM)
    dma = pltpu.SemaphoreType.DMA
    head_rows = jax.ShapeDtypeStruct((rows, HEAD_SIZE), bf16)
    grads = [
        jax.ShapeDtypeStruct(queries.shape, bf16),
        jax.ShapeDtypeStruct(key_states.shape, bf16),
        jax.ShapeDtypeStruct(key_states.shape, bf16),
    ]
    low_rows = pltpu.VMEM((rows, HEAD_SIZE), bf16)
    full_rows = pltpu.VMEM((rows, HEAD_SIZE), f32)

    if groups == 1:
        out = pl.pallas_call(
            functools.partial(fused_kernel, spans, ka_count),
            out_shape=grads,
            in_specs=[pl.BlockSpec(memory_space=pltpu.SMEM), vmem] + [any_space] * 4,
            out_specs=[any_space] * 3,
            scratch_shapes=[low_rows] * 4
            + [
                full_rows,
                pltpu.VMEM((HEAD_SIZE, rows), bf16),
                pltpu.VMEM((rows, TILE), f32),
                pltpu.VMEM((rows, TILE), f32),
                low_rows,
                full_rows,
                full_rows,
                full_rows,
                low_rows,
                dma,
                dma,
                dma((2,)),
                dma((2, spans)),
                dma,
                dma,
                dma,
                dma((spans,)),
                dma,
                dma,
                dma,
                dma((2,)),
            ],
            compiler_params=pltpu.CompilerParams(
                collective_id=2, has_side_effects=True, vmem_limit_bytes=VMEM_LIMIT
            ),
            name="heads_backward",
        )(
            listed.reshape(-1),
            turn_ids.astype(f32)[None, :],
            queries,
            output_gradient,
            key_states,
            value_inputs,
        )
        return tuple(part.astype(f32) for part in out)

    q, do, k, v = pl.pallas_call(
        functools.partial(gather_kernel, spans, ka_count),
        out_shape=[head_rows] * 4,
        in_specs=[any_space] * 4,
        out_specs=[any_space] * 4,
        scratch_shapes=[dma, dma, dma((2,)), dma((2, spans)), dma, dma],
        compiler_params=pltpu.CompilerParams(collective_id=0, has_side_effects=True),
        name="gather_heads",
    )(queries, output_gradient, key_states, value_inputs)

    group = lax.axis_index("pb") // spans
    turn_own = lax.dynamic_slice_in_dim(turn_ids, group * rows, rows, 0)
    turn_before = lax.dynamic_slice_in_dim(turn_ids, jnp.maximum(group - 1, 0) * rows, rows, 0)
    turn_before = jnp.where(group > 0, turn_before, NO_KEY)
    turn_keys = jnp.concatenate([turn_before, turn_own])
    forward = [(i, i + spans) for i in range(pb_count - spans)]
    k_before, v_before = lax.ppermute(jnp.stack([k, v]), "pb", forward)
    k = jnp.concatenate([k_before, k])
    v = jnp.concatenate([v_before, v])
    keys = halo + rows
    key_grad = jax.ShapeDtypeStruct((keys, HEAD_SIZE), f32)
    dq, dk, dv = pl.pallas_call(
        functools.partial(attention_kernel, spans, ka_count, halo),
        out_shape=[head_rows, key_grad, key_grad],
        in_specs=[pl.BlockSpec(memory_space=pltpu.SMEM)] + [vmem] * 6,
        out_specs=[vmem] * 3,
        scratch_shapes=[
            pltpu.VMEM((HEAD_SIZE, keys), bf16),
            pltpu.VMEM((keys, TILE), f32),
            pltpu.VMEM((keys, TILE), f32),
        ],
        compiler_params=pltpu.CompilerParams(vmem_limit_bytes=VMEM_LIMIT),
        name="attention_backward",
    )(
        listed.reshape(-1),
        turn_own.astype(f32)[None, :],
        jnp.broadcast_to(turn_keys.astype(f32)[:, None], (keys, HEAD_SIZE)),
        q,
        do,
        k,
        v,
    )
    back = [(i + spans, i) for i in range(pb_count - spans)]
    dk_later, dv_later = lax.ppermute(jnp.stack([dk[:halo], dv[:halo]]), "pb", back)
    dk = dk[halo:] + dk_later
    dv = dv[halo:] + dv_later

    out = pl.pallas_call(
        functools.partial(scatter_kernel, spans, ka_count),
        out_shape=grads,
        in_specs=[vmem] * 3,
        out_specs=[any_space] * 3,
        scratch_shapes=[
            pltpu.VMEM((rows, HEAD_SIZE), f32),
            pltpu.VMEM((rows, HEAD_SIZE), bf16),
            dma,
            dma,
            dma,
            dma,
            dma,
            dma((2,)),
        ],
        compiler_params=pltpu.CompilerParams(
            collective_id=1, has_side_effects=True, vmem_limit_bytes=VMEM_LIMIT
        ),
        name="scatter_gradients",
    )(dq, dk, dv)
    return tuple(part.astype(f32) for part in out)


def solution(mesh):
    in_specs = (
        P("pb", "ka"),
        P("pb", "ka"),
        P(("pb", "ka"), None),
        P(("pb", "ka"), None),
        P(),
        P(),
    )
    out_specs = (P("pb", "ka"), P(("pb", "ka"), None), P(("pb", "ka"), None))
    return jax.shard_map(
        per_device, mesh=mesh, in_specs=in_specs, out_specs=out_specs, check_vma=False
    )
```

```python
import functools

import jax
import jax.numpy as jnp
from jax import lax
from jax.experimental import pallas as pl
from jax.experimental.pallas import tpu as pltpu
from jax.sharding import PartitionSpec as P

QUERY_HEADS = 32
KEY_VALUE_HEADS = 16
HEAD_SIZE = 128
HEAD_GROUPS = 2
BLOCK_POSITIONS = 128
BACK = 14

SCORE_SCALE = 1.0 / 12.0
LOG2E = 1.4426950408889634
NEG_LARGE = -1e30
HIT = float(1 << 20)
NO_KEY = -(1 << 22)
TILE = 256
MESH = pl.DeviceIdType.MESH
VMEM_LIMIT = 48 * 1024 * 1024
FUSED_VMEM_LIMIT = 60 * 1024 * 1024


class Place:
    def __init__(self, spans, ka_count):
        self.spans = spans
        self.ka_count = ka_count
        pb = lax.axis_index("pb")
        self.ka = lax.axis_index("ka")
        self.group = pb // spans
        self.span = pb % spans
        self.pair = self.ka // 2
        self.core = self.ka % 2
        self.head = self.pair * spans + self.span
        self.held = KEY_VALUE_HEADS // ka_count

    def at(self, span, ka):
        return {"pb": self.group * self.spans + span, "ka": ka}

    def greet(self):
        barrier = pltpu.get_barrier_semaphore()
        for t in range(1, self.spans * self.ka_count):
            pl.semaphore_signal(
                barrier,
                inc=1,
                device_id=self.at(
                    (self.span + t // self.ka_count) % self.spans,
                    (self.ka + t % self.ka_count) % self.ka_count,
                ),
                device_id_type=MESH,
            )
        pl.semaphore_wait(barrier, self.spans * self.ka_count - 1)


def wait_for(ref, sem):
    pltpu.make_async_copy(ref, ref, sem).wait()


def lanes(index):
    return pl.ds(pl.multiple_of(index * HEAD_SIZE, HEAD_SIZE), HEAD_SIZE)


def rows_at(begin, count):
    return pl.ds(pl.multiple_of(begin, count), count)


def send_heads(me, q, do, k, v, qh, doh, kh, vh, kv_send, kv_recv, q_send, q_recv):
    tok = q.shape[0]
    piece = k.shape[0]
    kv_rows = rows_at(me.span * tok + me.ka * piece, piece)
    for t in range(me.spans * me.ka_count // 2):
        span = (me.span + t % me.spans) % me.spans
        pair = (me.pair + t // me.spans) % (me.ka_count // 2)
        cols = lanes(pair * me.spans + span)
        for core, (src, dst) in enumerate(((k, kh), (v, vh))):

            def remote(src=src, dst=dst, core=core, span=span, pair=pair, cols=cols):
                pltpu.make_async_remote_copy(
                    src_ref=src.at[:, cols],
                    dst_ref=dst.at[kv_rows, :],
                    send_sem=kv_send,
                    recv_sem=kv_recv,
                    device_id=me.at(span, 2 * pair + core),
                    device_id_type=MESH,
                ).start()

            if t == 0:
                pl.when(me.core != core)(remote)

                @pl.when(me.core == core)
                def _(src=src, dst=dst, cols=cols):
                    pltpu.make_async_copy(src.at[:, cols], dst.at[kv_rows, :], kv_recv).start()
            else:
                remote()
    q_rows = rows_at(me.span * tok, tok)
    for j in range(me.held):
        near = (me.span + j) % me.held
        span = me.held * me.core + near
        for core in range(2):
            cols = lanes(2 * near + core)
            mine = (span == me.span) & (me.core == core)
            for which, (src, dst) in enumerate(((q, qh), (do, doh))):
                sem = q_recv.at[which, me.span]

                @pl.when(mine)
                def _(src=src, dst=dst, cols=cols, sem=sem):
                    pltpu.make_async_copy(src.at[:, cols], dst.at[q_rows, :], sem).start()

                @pl.when(jnp.logical_not(mine))
                def _(src=src, dst=dst, cols=cols, core=core, span=span, which=which, sem=sem):
                    pltpu.make_async_remote_copy(
                        src_ref=src.at[:, cols],
                        dst_ref=dst.at[q_rows, :],
                        send_sem=q_send.at[which],
                        recv_sem=sem,
                        device_id=me.at(span, 2 * me.pair + core),
                        device_id_type=MESH,
                    ).start()


def to_other_core(me, src, dst, send_sem, recv_sem):
    return pltpu.make_async_remote_copy(
        src_ref=src,
        dst_ref=dst,
        send_sem=send_sem,
        recv_sem=recv_sem,
        device_id=me.at(me.span, 2 * me.pair + 1 - me.core),
        device_id_type=MESH,
    )


def share_keys(me, kh, vh, kv_recv, x_send, x_recv):
    for core, ref in enumerate((kh, vh)):

        @pl.when(me.core == core)
        def _(ref=ref):
            wait_for(ref, kv_recv)
            to_other_core(me, ref, ref, x_send, x_recv).start()

    wait_for(kh, x_recv)


def finish_heads(me, qh, doh, kh, kv_send, q_send, x_send, tok, piece):
    wait_for(kh, x_send)
    wait_for(kh.at[: (me.spans * me.ka_count - 1) * piece], kv_send)
    sent = 2 * me.held * tok
    has_own = me.span // me.held == me.core
    for which, ref in enumerate((qh, doh)):
        sem = q_send.at[which]
        pl.when(has_own)(lambda ref=ref, sem=sem: wait_for(ref.at[: sent - tok], sem))
        pl.when(jnp.logical_not(has_own))(lambda ref=ref, sem=sem: wait_for(ref.at[:sent], sem))


def gather_kernel(
    spans, ka_count, q, do, k, v, qh, doh, kh, vh, kv_send, kv_recv, q_send, q_recv, x_send, x_recv
):
    me = Place(spans, ka_count)
    tok = q.shape[0]
    me.greet()
    send_heads(me, q, do, k, v, qh, doh, kh, vh, kv_send, kv_recv, q_send, q_recv)
    share_keys(me, kh, vh, kv_recv, x_send, x_recv)
    for span in range(spans):
        wait_for(qh.at[span * tok : (span + 1) * tok], q_recv.at[0, span])
        wait_for(doh.at[span * tok : (span + 1) * tok], q_recv.at[1, span])
    finish_heads(me, qh, doh, kh, kv_send, q_send, x_send, tok, k.shape[0])


def fused_kernel(
    spans, ka_count, listed, turn_row, q, do, k, v, dq, dk, dv,
    qh, doh, kh, vh, turn_col, kt, s_buf, g_buf, dqh, dkh, dvh, got, low,
    kv_send, kv_recv, q_send, q_recv, k_send, k_recv,
    x_send, x_recv, dq_send, dq_recv, dkv_send, dkv_recv,
):
    me = Place(spans, ka_count)
    tok = q.shape[0]
    piece = k.shape[0]
    me.greet()
    send_heads(me, q, do, k, v, qh, doh, kh, vh, kv_send, kv_recv, q_send, q_recv)
    for n in range(turn_col.shape[0] // HEAD_SIZE):
        at = slice(n * HEAD_SIZE, (n + 1) * HEAD_SIZE)
        turns = turn_row[:, at].astype(jnp.float32)
        turn_col[at, :] = jnp.broadcast_to(turns, (HEAD_SIZE, HEAD_SIZE)).T
    share_keys(me, kh, vh, kv_recv, k_send, k_recv)
    owner = 2 * me.pair + me.span // me.held
    q_cols = lanes(2 * (me.span % me.held) + me.core)
    head_cols = lanes(me.head)

    def ready(i):
        wait_for(qh.at[i * tok : (i + 1) * tok], q_recv.at[0, i])
        wait_for(doh.at[i * tok : (i + 1) * tok], q_recv.at[1, i])

    def in_turn(batch):
        return [batch[0] + (me.span + t) % len(batch) for t in range(len(batch))]

    def send_queries(batch):
        for span in in_turn(batch):
            src = dqh.at[rows_at(span * tok, tok), :]
            mine = (me.span == span) & (owner == me.ka)

            @pl.when(mine)
            def _(src=src):
                pltpu.make_async_copy(src, dq.at[:, q_cols], dq_recv).start()

            @pl.when(jnp.logical_not(mine))
            def _(src=src, span=span):
                pltpu.make_async_remote_copy(
                    src_ref=src,
                    dst_ref=dq.at[:, q_cols],
                    send_sem=dq_send,
                    recv_sem=dq_recv,
                    device_id=me.at(span, owner),
                    device_id_type=MESH,
                ).start()

    def share_grads(j):
        at = slice(j * tok, (j + 1) * tok)
        for core, ref in enumerate((dvh, dkh)):

            @pl.when(me.core == core)
            def _(ref=ref):
                to_other_core(me, ref.at[at], got.at[at], x_send, x_recv.at[j]).start()

    def send_grads(batch):
        for j in batch:
            wait_for(got.at[j * tok : (j + 1) * tok], x_recv.at[j])
        for core, (own, out) in enumerate(((dkh, dk), (dvh, dv))):

            @pl.when(me.core == core)
            def _(own=own, out=out, core=core):
                at = slice(batch[0] * tok, (batch[-1] + 1) * tok)
                low[at, :] = (own[at, :] + got[at, :]).astype(jnp.bfloat16)
                for span in in_turn(batch):
                    for t in range(ka_count):
                        ka = (me.ka + t) % ka_count
                        src = low.at[rows_at(span * tok + ka * piece, piece), :]
                        dst = out.at[:, head_cols]

                        def remote(src=src, dst=dst, ka=ka, span=span):
                            pltpu.make_async_remote_copy(
                                src_ref=src,
                                dst_ref=dst,
                                send_sem=dkv_send,
                                recv_sem=dkv_recv.at[core],
                                device_id=me.at(span, ka),
                                device_id_type=MESH,
                            ).start()

                        if t == 0:
                            pl.when(me.span != span)(remote)

                            @pl.when(me.span == span)
                            def _(src=src, dst=dst):
                                pltpu.make_async_copy(src, dst, dkv_recv.at[core]).start()
                        else:
                            remote()

    half = spans // 2
    top = spans - 1
    order = [top, *range(half), *range(top - 1, half - 1, -1)]
    query_batches = {top: [top], half - 1: list(range(half)), top - 1: [top - 1]}
    query_batches[half] = list(range(half, top - 1))
    grad_batches = {0: [top], top - 2: [top - 1]}
    shares = {top: [top], top - 1: [top - 1], top - 2: [top - 2]}
    shares[half] = list(range(top - 3, -1, -1))

    def after(i):
        for j in shares.get(i, []):
            share_grads(j)
        if i in query_batches:
            send_queries(query_batches[i])
        if i in grad_batches:
            send_grads(grad_batches[i])

    attend(
        me, 0, order, ready, after,
        listed, turn_row, turn_col, qh, doh, kh, vh, dqh, dkh, dvh, kt, s_buf, g_buf,
    )
    send_grads(list(range(top - 1)))
    finish_heads(me, qh, doh, kh, kv_send, q_send, k_send, tok, piece)
    wait_for(got, x_send)
    sent = spans * tok
    pl.when(owner == me.ka)(lambda: wait_for(dqh.at[: sent - tok], dq_send))
    pl.when(owner != me.ka)(lambda: wait_for(dqh.at[:sent], dq_send))
    wait_for(low.at[: (spans * ka_count - 1) * piece], dkv_send)
    wait_for(dq, dq_recv)
    wait_for(dk, dkv_recv.at[0])
    wait_for(dv, dkv_recv.at[1])


def attention_kernel(spans, ka_count, halo, *refs):
    order = list(range(refs[3].shape[0] // TILE))
    nothing = lambda i: None
    attend(Place(spans, ka_count), halo, order, nothing, nothing, *refs)


def attend(
    me, halo, order, ready, after,
    listed, turn_row, turn_col, q, do, k, v, dq, dk, dv, kt, s_buf, g_buf,
):
    rows = q.shape[0]
    keys = k.shape[0]
    blocks = listed.shape[0] // (HEAD_GROUPS * BACK)
    head_group = me.head // (KEY_VALUE_HEADS // HEAD_GROUPS)
    list_base = (head_group * blocks + me.group * (rows // BLOCK_POSITIONS)) * BACK
    dk[...] = jnp.zeros_like(dk)
    dv[...] = jnp.zeros_like(dv)
    for n in range(keys // TILE):
        kt[:, n * TILE : (n + 1) * TILE] = k[n * TILE : (n + 1) * TILE, :].T
    left = lax.broadcasted_iota(jnp.int32, (1, TILE), 1) < BLOCK_POSITIONS
    causal = lax.broadcasted_iota(jnp.int32, (TILE, TILE), 0) <= lax.broadcasted_iota(
        jnp.int32, (TILE, TILE), 1
    )

    def hit(block, key_block):
        offset = block - key_block - 1
        if 0 <= offset < BACK:
            return listed[list_base + block * BACK + offset]
        return jnp.int32(0)

    for i in order:
        ready(i)
        q_i = q[i * TILE : (i + 1) * TILE, :]
        do_i = do[i * TILE : (i + 1) * TILE, :]
        turn_i = turn_row[:, i * TILE : (i + 1) * TILE].astype(jnp.float32)
        last = halo // TILE + i
        first = max(0, last - BACK * BLOCK_POSITIONS // TILE)
        peak = jnp.full((8, TILE), NEG_LARGE, jnp.float32)
        for n in range(first, last + 1):
            at = slice(n * TILE, (n + 1) * TILE)
            s = lax.dot_general(
                k[at, :], q_i, (((1,), (1,)), ((), ())), preferred_element_type=jnp.float32
            ) * (SCORE_SCALE * LOG2E)
            parts = []
            for half in range(TILE // BLOCK_POSITIONS):
                key_block = 2 * n + half - halo // BLOCK_POSITIONS
                seen = jnp.where(left, hit(2 * i, key_block), hit(2 * i + 1, key_block))
                bar = turn_i - seen.astype(jnp.float32) * HIT
                begin = n * TILE + half * BLOCK_POSITIONS
                turns = turn_col[begin : begin + BLOCK_POSITIONS, :]
                parts.append(jnp.concatenate([turns, turns], axis=1) >= bar)
            allowed = jnp.concatenate(parts, axis=0)
            if n == last:
                allowed = allowed & causal
            s = jnp.where(allowed, s, NEG_LARGE)
            s_buf[at, :] = s
            peak = jnp.maximum(peak, jnp.max(s.reshape(TILE // 8, 8, TILE), axis=0))
        peak = jnp.max(peak, axis=0, keepdims=True)
        total = jnp.zeros((8, TILE), jnp.float32)
        inner = jnp.zeros((8, TILE), jnp.float32)
        for n in range(first, last + 1):
            at = slice(n * TILE, (n + 1) * TILE)
            g = lax.dot_general(
                v[at, :], do_i, (((1,), (1,)), ((), ())), preferred_element_type=jnp.float32
            )
            p = jnp.exp2(s_buf[at, :] - peak)
            s_buf[at, :] = p
            g_buf[at, :] = g
            total = total + jnp.sum(p.reshape(TILE // 8, 8, TILE), axis=0)
            inner = inner + jnp.sum((p * g).reshape(TILE // 8, 8, TILE), axis=0)
        inverse = 1.0 / jnp.sum(total, axis=0, keepdims=True)
        delta = jnp.sum(inner, axis=0, keepdims=True) * inverse
        scaled = inverse * SCORE_SCALE
        dq_t = jnp.zeros((HEAD_SIZE, TILE), jnp.float32)
        for n in range(first, last + 1):
            at = slice(n * TILE, (n + 1) * TILE)
            p = s_buf[at, :]
            mixed = ((p * scaled) * (g_buf[at, :] - delta)).astype(jnp.bfloat16)
            low = (p * inverse).astype(jnp.bfloat16)
            dv[at, :] += jnp.dot(low, do_i, preferred_element_type=jnp.float32)
            dk[at, :] += jnp.dot(mixed, q_i, preferred_element_type=jnp.float32)
            dq_t = dq_t + jnp.dot(kt[:, at], mixed, preferred_element_type=jnp.float32)
        dq[i * TILE : (i + 1) * TILE, :] = dq_t.T.astype(jnp.bfloat16)
        after(i)


def scatter_kernel(
    spans, ka_count, dqh, dkh, dvh, dq, dk, dv, got, low, x_send, x_recv, q_send, q_recv, kv_send, kv_recv
):
    me = Place(spans, ka_count)
    tok = dq.shape[0]
    piece = dk.shape[0]
    me.greet()

    def exchange(ref):
        return pltpu.make_async_remote_copy(
            src_ref=ref,
            dst_ref=got,
            send_sem=x_send,
            recv_sem=x_recv,
            device_id=me.at(me.span, 2 * me.pair + 1 - me.core),
            device_id_type=MESH,
        )

    pl.when(me.core == 0)(lambda: exchange(dvh).start())
    pl.when(me.core == 1)(lambda: exchange(dkh).start())
    owner = 2 * me.pair + me.span // me.held
    cols = lanes(2 * (me.span % me.held) + me.core)
    for t in range(spans):
        span = (me.span + t) % spans
        src = dqh.at[rows_at(span * tok, tok), :]

        def remote(src=src, span=span):
            pltpu.make_async_remote_copy(
                src_ref=src,
                dst_ref=dq.at[:, cols],
                send_sem=q_send,
                recv_sem=q_recv,
                device_id=me.at(span, owner),
                device_id_type=MESH,
            ).start()

        if t == 0:
            pl.when(owner != me.ka)(remote)

            @pl.when(owner == me.ka)
            def _(src=src):
                pltpu.make_async_copy(src, dq.at[:, cols], q_recv).start()
        else:
            remote()
    wait_for(got, x_recv)
    for core, (own, out) in enumerate(((dkh, dk), (dvh, dv))):

        @pl.when(me.core == core)
        def _(own=own, out=out):
            low[...] = (own[...] + got[...]).astype(jnp.bfloat16)
            head_cols = lanes(me.head)
            for t in range(spans * ka_count):
                span = (me.span + t // ka_count) % spans
                ka = (me.ka + t % ka_count) % ka_count
                src = low.at[rows_at(span * tok + ka * piece, piece), :]
                dst = out.at[:, head_cols]
                if t == 0:
                    pltpu.make_async_copy(src, dst, kv_recv.at[core]).start()
                else:
                    pltpu.make_async_remote_copy(
                        src_ref=src,
                        dst_ref=dst,
                        send_sem=kv_send,
                        recv_sem=kv_recv.at[core],
                        device_id=me.at(span, ka),
                        device_id_type=MESH,
                    ).start()

    wait_for(got, x_send)
    sent = spans * tok
    pl.when(owner == me.ka)(lambda: wait_for(dqh.at[: sent - tok], q_send))
    pl.when(owner != me.ka)(lambda: wait_for(dqh.at[:sent], q_send))
    wait_for(dq, q_recv)
    wait_for(low.at[: (spans * ka_count - 1) * piece], kv_send)
    wait_for(dk, kv_recv.at[0])
    wait_for(dv, kv_recv.at[1])


def per_device(queries, output_gradient, key_states, value_inputs, turn_ids, listed):
    ka_count = lax.axis_size("ka")
    pb_count = lax.axis_size("pb")
    spans = 2 * KEY_VALUE_HEADS // ka_count
    groups = pb_count // spans
    tok = queries.shape[0]
    piece = key_states.shape[0]
    rows = spans * tok
    halo = rows
    bf16, f32 = jnp.bfloat16, jnp.float32
    any_space = pl.BlockSpec(memory_space=pl.ANY)
    vmem = pl.BlockSpec(memory_space=pltpu.VMEM)
    dma = pltpu.SemaphoreType.DMA
    head_rows = jax.ShapeDtypeStruct((rows, HEAD_SIZE), bf16)
    grads = [
        jax.ShapeDtypeStruct(queries.shape, bf16),
        jax.ShapeDtypeStruct(key_states.shape, bf16),
        jax.ShapeDtypeStruct(key_states.shape, bf16),
    ]
    low_rows = pltpu.VMEM((rows, HEAD_SIZE), bf16)
    full_rows = pltpu.VMEM((rows, HEAD_SIZE), f32)

    if groups == 1:
        out = pl.pallas_call(
            functools.partial(fused_kernel, spans, ka_count),
            out_shape=grads,
            in_specs=[pl.BlockSpec(memory_space=pltpu.SMEM), vmem]
            + [pl.BlockSpec(memory_space=pltpu.HBM)] * 4,
            out_specs=[any_space] * 3,
            scratch_shapes=[low_rows] * 4
            + [
                full_rows,
                pltpu.VMEM((HEAD_SIZE, rows), bf16),
                pltpu.VMEM((rows, TILE), f32),
                pltpu.VMEM((rows, TILE), f32),
                low_rows,
                full_rows,
                full_rows,
                full_rows,
                low_rows,
                dma,
                dma,
                dma((2,)),
                dma((2, spans)),
                dma,
                dma,
                dma,
                dma((spans,)),
                dma,
                dma,
                dma,
                dma((2,)),
            ],
            compiler_params=pltpu.CompilerParams(
                collective_id=2, has_side_effects=True, vmem_limit_bytes=FUSED_VMEM_LIMIT
            ),
            name="heads_backward",
        )(
            listed.reshape(-1),
            turn_ids[None, :],
            queries,
            output_gradient,
            key_states,
            value_inputs,
        )
        return tuple(part.astype(f32) for part in out)

    q, do, k, v = pl.pallas_call(
        functools.partial(gather_kernel, spans, ka_count),
        out_shape=[head_rows] * 4,
        in_specs=[any_space] * 4,
        out_specs=[any_space] * 4,
        scratch_shapes=[dma, dma, dma((2,)), dma((2, spans)), dma, dma],
        compiler_params=pltpu.CompilerParams(collective_id=0, has_side_effects=True),
        name="gather_heads",
    )(queries, output_gradient, key_states, value_inputs)

    group = lax.axis_index("pb") // spans
    turn_own = lax.dynamic_slice_in_dim(turn_ids, group * rows, rows, 0)
    turn_before = lax.dynamic_slice_in_dim(turn_ids, jnp.maximum(group - 1, 0) * rows, rows, 0)
    turn_before = jnp.where(group > 0, turn_before, NO_KEY)
    turn_keys = jnp.concatenate([turn_before, turn_own])
    forward = [(i, i + spans) for i in range(pb_count - spans)]
    k_before, v_before = lax.ppermute(jnp.stack([k, v]), "pb", forward)
    k = jnp.concatenate([k_before, k])
    v = jnp.concatenate([v_before, v])
    keys = halo + rows
    key_grad = jax.ShapeDtypeStruct((keys, HEAD_SIZE), f32)
    dq, dk, dv = pl.pallas_call(
        functools.partial(attention_kernel, spans, ka_count, halo),
        out_shape=[head_rows, key_grad, key_grad],
        in_specs=[pl.BlockSpec(memory_space=pltpu.SMEM)] + [vmem] * 6,
        out_specs=[vmem] * 3,
        scratch_shapes=[
            pltpu.VMEM((HEAD_SIZE, keys), bf16),
            pltpu.VMEM((keys, TILE), f32),
            pltpu.VMEM((keys, TILE), f32),
        ],
        compiler_params=pltpu.CompilerParams(vmem_limit_bytes=VMEM_LIMIT),
        name="attention_backward",
    )(
        listed.reshape(-1),
        turn_own.astype(f32)[None, :],
        jnp.broadcast_to(turn_keys.astype(f32)[:, None], (keys, HEAD_SIZE)),
        q,
        do,
        k,
        v,
    )
    back = [(i + spans, i) for i in range(pb_count - spans)]
    dk_later, dv_later = lax.ppermute(jnp.stack([dk[:halo], dv[:halo]]), "pb", back)
    dk = dk[halo:] + dk_later
    dv = dv[halo:] + dv_later

    out = pl.pallas_call(
        functools.partial(scatter_kernel, spans, ka_count),
        out_shape=grads,
        in_specs=[vmem] * 3,
        out_specs=[any_space] * 3,
        scratch_shapes=[
            pltpu.VMEM((rows, HEAD_SIZE), f32),
            pltpu.VMEM((rows, HEAD_SIZE), bf16),
            dma,
            dma,
            dma,
            dma,
            dma,
            dma((2,)),
        ],
        compiler_params=pltpu.CompilerParams(
            collective_id=1, has_side_effects=True, vmem_limit_bytes=VMEM_LIMIT
        ),
        name="scatter_gradients",
    )(dq, dk, dv)
    return tuple(part.astype(f32) for part in out)


def solution(mesh):
    in_specs = (
        P("pb", "ka"),
        P("pb", "ka"),
        P(("pb", "ka"), None),
        P(("pb", "ka"), None),
        P(),
        P(),
    )
    out_specs = (P("pb", "ka"), P(("pb", "ka"), None), P(("pb", "ka"), None))
    return jax.shard_map(
        per_device, mesh=mesh, in_specs=in_specs, out_specs=out_specs, check_vma=False
    )
```

```python
import functools

import jax
import jax.numpy as jnp
from jax import lax
from jax.experimental import pallas as pl
from jax.experimental.pallas import tpu as pltpu
from jax.sharding import PartitionSpec as P

QUERY_HEADS = 32
KEY_VALUE_HEADS = 16
HEAD_SIZE = 128
HEAD_GROUPS = 2
BLOCK_POSITIONS = 128
BACK = 14

SCORE_SCALE = 1.0 / 12.0
LOG2E = 1.4426950408889634
NEG_LARGE = -1e30
HIT = float(1 << 20)
NO_KEY = -(1 << 22)
TILE = 256
MESH = pl.DeviceIdType.MESH
VMEM_LIMIT = 48 * 1024 * 1024
FUSED_VMEM_LIMIT = 60 * 1024 * 1024


class Place:
    def __init__(self, spans, ka_count):
        self.spans = spans
        self.ka_count = ka_count
        pb = lax.axis_index("pb")
        self.ka = lax.axis_index("ka")
        self.group = pb // spans
        self.span = pb % spans
        self.pair = self.ka // 2
        self.core = self.ka % 2
        self.head = self.pair * spans + self.span
        self.held = KEY_VALUE_HEADS // ka_count

    def at(self, span, ka):
        return {"pb": self.group * self.spans + span, "ka": ka}

    def greet(self):
        barrier = pltpu.get_barrier_semaphore()
        for t in range(1, self.spans * self.ka_count):
            pl.semaphore_signal(
                barrier,
                inc=1,
                device_id=self.at(
                    (self.span + t // self.ka_count) % self.spans,
                    (self.ka + t % self.ka_count) % self.ka_count,
                ),
                device_id_type=MESH,
            )
        pl.semaphore_wait(barrier, self.spans * self.ka_count - 1)


def wait_for(ref, sem):
    pltpu.make_async_copy(ref, ref, sem).wait()


def lanes(index):
    return pl.ds(pl.multiple_of(index * HEAD_SIZE, HEAD_SIZE), HEAD_SIZE)


def rows_at(begin, count):
    return pl.ds(pl.multiple_of(begin, count), count)


def send_heads(me, q, do, k, v, qh, doh, kh, vh, kv_send, kv_recv, q_send, q_recv):
    tok = q.shape[0]
    piece = k.shape[0]
    kv_rows = rows_at(me.span * tok + me.ka * piece, piece)
    for t in range(me.spans * me.ka_count // 2):
        span = (me.span + t % me.spans) % me.spans
        pair = (me.pair + t // me.spans) % (me.ka_count // 2)
        cols = lanes(pair * me.spans + span)
        for core, (src, dst) in enumerate(((k, kh), (v, vh))):

            def remote(src=src, dst=dst, core=core, span=span, pair=pair, cols=cols):
                pltpu.make_async_remote_copy(
                    src_ref=src.at[:, cols],
                    dst_ref=dst.at[kv_rows, :],
                    send_sem=kv_send,
                    recv_sem=kv_recv,
                    device_id=me.at(span, 2 * pair + core),
                    device_id_type=MESH,
                ).start()

            if t == 0:
                pl.when(me.core != core)(remote)

                @pl.when(me.core == core)
                def _(src=src, dst=dst, cols=cols):
                    pltpu.make_async_copy(src.at[:, cols], dst.at[kv_rows, :], kv_recv).start()
            else:
                remote()
    q_rows = rows_at(me.span * tok, tok)
    for j in range(me.held):
        near = (me.span + j) % me.held
        span = me.held * me.core + near
        for core in range(2):
            cols = lanes(2 * near + core)
            mine = (span == me.span) & (me.core == core)
            for which, (src, dst) in enumerate(((q, qh), (do, doh))):
                sem = q_recv.at[which, me.span]

                @pl.when(mine)
                def _(src=src, dst=dst, cols=cols, sem=sem):
                    pltpu.make_async_copy(src.at[:, cols], dst.at[q_rows, :], sem).start()

                @pl.when(jnp.logical_not(mine))
                def _(src=src, dst=dst, cols=cols, core=core, span=span, which=which, sem=sem):
                    pltpu.make_async_remote_copy(
                        src_ref=src.at[:, cols],
                        dst_ref=dst.at[q_rows, :],
                        send_sem=q_send.at[which],
                        recv_sem=sem,
                        device_id=me.at(span, 2 * me.pair + core),
                        device_id_type=MESH,
                    ).start()


def to_other_core(me, src, dst, send_sem, recv_sem):
    return pltpu.make_async_remote_copy(
        src_ref=src,
        dst_ref=dst,
        send_sem=send_sem,
        recv_sem=recv_sem,
        device_id=me.at(me.span, 2 * me.pair + 1 - me.core),
        device_id_type=MESH,
    )


def share_keys(me, kh, vh, kv_recv, x_send, x_recv):
    for core, ref in enumerate((kh, vh)):

        @pl.when(me.core == core)
        def _(ref=ref):
            wait_for(ref, kv_recv)
            to_other_core(me, ref, ref, x_send, x_recv).start()

    wait_for(kh, x_recv)


def finish_heads(me, qh, doh, kh, kv_send, q_send, x_send, tok, piece):
    wait_for(kh, x_send)
    wait_for(kh.at[: (me.spans * me.ka_count - 1) * piece], kv_send)
    sent = 2 * me.held * tok
    has_own = me.span // me.held == me.core
    for which, ref in enumerate((qh, doh)):
        sem = q_send.at[which]
        pl.when(has_own)(lambda ref=ref, sem=sem: wait_for(ref.at[: sent - tok], sem))
        pl.when(jnp.logical_not(has_own))(lambda ref=ref, sem=sem: wait_for(ref.at[:sent], sem))


def gather_kernel(
    spans, ka_count, q, do, k, v, qh, doh, kh, vh, kv_send, kv_recv, q_send, q_recv, x_send, x_recv
):
    me = Place(spans, ka_count)
    tok = q.shape[0]
    me.greet()
    send_heads(me, q, do, k, v, qh, doh, kh, vh, kv_send, kv_recv, q_send, q_recv)
    share_keys(me, kh, vh, kv_recv, x_send, x_recv)
    for span in range(spans):
        wait_for(qh.at[span * tok : (span + 1) * tok], q_recv.at[0, span])
        wait_for(doh.at[span * tok : (span + 1) * tok], q_recv.at[1, span])
    finish_heads(me, qh, doh, kh, kv_send, q_send, x_send, tok, k.shape[0])


def fused_kernel(
    spans, ka_count, listed, turn_row, q, do, k, v, dq, dk, dv,
    qh, doh, kh, vh, turn_col, kt, s_buf, g_buf, dqh, dkh, dvh, got, low,
    kv_send, kv_recv, q_send, q_recv, k_send, k_recv,
    x_send, x_recv, dq_send, dq_recv, dkv_send, dkv_recv,
):
    me = Place(spans, ka_count)
    tok = q.shape[0]
    piece = k.shape[0]
    me.greet()
    send_heads(me, q, do, k, v, qh, doh, kh, vh, kv_send, kv_recv, q_send, q_recv)
    for n in range(turn_col.shape[0] // HEAD_SIZE):
        at = slice(n * HEAD_SIZE, (n + 1) * HEAD_SIZE)
        turns = turn_row[:, at].astype(jnp.float32)
        turn_col[at, :] = jnp.broadcast_to(turns, (HEAD_SIZE, HEAD_SIZE)).T
    share_keys(me, kh, vh, kv_recv, k_send, k_recv)
    owner = 2 * me.pair + me.span // me.held
    q_cols = lanes(2 * (me.span % me.held) + me.core)
    head_cols = lanes(me.head)

    def ready(span):
        for which, ref in enumerate((qh, doh)):
            wait_for(ref.at[rows_at(span * tok, tok), :], q_recv.at[which, span])

    def send_queries(span):
        src = dqh.at[rows_at(span * tok, tok), :]
        mine = (me.span == span) & (owner == me.ka)

        @pl.when(mine)
        def _():
            pltpu.make_async_copy(src, dq.at[:, q_cols], dq_recv).start()

        @pl.when(jnp.logical_not(mine))
        def _():
            pltpu.make_async_remote_copy(
                src_ref=src,
                dst_ref=dq.at[:, q_cols],
                send_sem=dq_send,
                recv_sem=dq_recv,
                device_id=me.at(span, owner),
                device_id_type=MESH,
            ).start()

    tile = attend(me, 0, listed, turn_row, turn_col, qh, doh, kh, vh, dqh, dkh, dvh, kt, s_buf, g_buf)

    def query_step(t, carry):
        span = (me.span + me.held - t // 2) % me.held
        span = span + me.held * ((t + me.span // me.held) % 2)
        ready(span)
        for i in range(spans):
            pl.when(span == i)(functools.partial(tile, i))
        send_queries(span)
        return carry

    lax.fori_loop(0, spans, query_step, 0)

    def share_step(t, carry):
        span = (me.span + t) % spans
        at = rows_at(span * tok, tok)
        for core, ref in enumerate((dvh, dkh)):

            @pl.when(me.core == core)
            def _(ref=ref):
                to_other_core(
                    me, ref.at[at, :], got.at[at, :], x_send, x_recv.at[span]
                ).start()

        return carry

    lax.fori_loop(0, spans, share_step, 0)

    def grad_step(t, carry):
        span = (me.span + t) % spans
        at = rows_at(span * tok, tok)
        wait_for(got.at[at, :], x_recv.at[span])
        for core, (own, out) in enumerate(((dkh, dk), (dvh, dv))):

            @pl.when(me.core == core)
            def _(own=own, out=out, core=core):
                low[at, :] = (own[at, :] + got[at, :]).astype(jnp.bfloat16)
                dst = out.at[:, head_cols]
                for n in range(ka_count):
                    ka = (me.ka + n) % ka_count
                    src = low.at[rows_at(span * tok + ka * piece, piece), :]

                    def remote(src=src, ka=ka):
                        pltpu.make_async_remote_copy(
                            src_ref=src,
                            dst_ref=dst,
                            send_sem=dkv_send,
                            recv_sem=dkv_recv.at[core],
                            device_id=me.at(span, ka),
                            device_id_type=MESH,
                        ).start()

                    if n == 0:
                        pl.when(me.span != span)(remote)

                        @pl.when(me.span == span)
                        def _(src=src):
                            pltpu.make_async_copy(src, dst, dkv_recv.at[core]).start()
                    else:
                        remote()

        return carry

    lax.fori_loop(0, spans, grad_step, 0)
    finish_heads(me, qh, doh, kh, kv_send, q_send, k_send, tok, piece)
    wait_for(got, x_send)
    sent = spans * tok
    pl.when(owner == me.ka)(lambda: wait_for(dqh.at[: sent - tok], dq_send))
    pl.when(owner != me.ka)(lambda: wait_for(dqh.at[:sent], dq_send))
    wait_for(low.at[: (spans * ka_count - 1) * piece], dkv_send)
    wait_for(dq, dq_recv)
    wait_for(dk, dkv_recv.at[0])
    wait_for(dv, dkv_recv.at[1])


def attention_kernel(spans, ka_count, halo, *refs):
    tile = attend(Place(spans, ka_count), halo, *refs)
    for i in range(refs[3].shape[0] // TILE):
        tile(i)


def attend(me, halo, listed, turn_row, turn_col, q, do, k, v, dq, dk, dv, kt, s_buf, g_buf):
    rows = q.shape[0]
    keys = k.shape[0]
    head_group = me.head // (KEY_VALUE_HEADS // HEAD_GROUPS)
    block_base = me.group * (rows // BLOCK_POSITIONS)
    dk[...] = jnp.zeros_like(dk)
    dv[...] = jnp.zeros_like(dv)
    for n in range(keys // TILE):
        kt[:, n * TILE : (n + 1) * TILE] = k[n * TILE : (n + 1) * TILE, :].T
    left = lax.broadcasted_iota(jnp.int32, (1, TILE), 1) < BLOCK_POSITIONS
    causal = lax.broadcasted_iota(jnp.int32, (TILE, TILE), 0) <= lax.broadcasted_iota(
        jnp.int32, (TILE, TILE), 1
    )

    def hit(block, key_block):
        offset = block - key_block - 1
        if 0 <= offset < BACK:
            return listed[head_group, block_base + block, offset]
        return jnp.int32(0)

    def tile(i):
        q_i = q[i * TILE : (i + 1) * TILE, :]
        do_i = do[i * TILE : (i + 1) * TILE, :]
        turn_i = turn_row[:, i * TILE : (i + 1) * TILE].astype(jnp.float32)
        last = halo // TILE + i
        first = max(0, last - BACK * BLOCK_POSITIONS // TILE)
        peak = jnp.full((8, TILE), NEG_LARGE, jnp.float32)
        for n in range(first, last + 1):
            at = slice(n * TILE, (n + 1) * TILE)
            s = lax.dot_general(
                k[at, :], q_i, (((1,), (1,)), ((), ())), preferred_element_type=jnp.float32
            ) * (SCORE_SCALE * LOG2E)
            parts = []
            for half in range(TILE // BLOCK_POSITIONS):
                key_block = 2 * n + half - halo // BLOCK_POSITIONS
                seen = jnp.where(left, hit(2 * i, key_block), hit(2 * i + 1, key_block))
                bar = turn_i - seen.astype(jnp.float32) * HIT
                begin = n * TILE + half * BLOCK_POSITIONS
                turns = turn_col[begin : begin + BLOCK_POSITIONS, :]
                parts.append(jnp.concatenate([turns, turns], axis=1) >= bar)
            allowed = jnp.concatenate(parts, axis=0)
            if n == last:
                allowed = allowed & causal
            s = jnp.where(allowed, s, NEG_LARGE)
            s_buf[at, :] = s
            peak = jnp.maximum(peak, jnp.max(s.reshape(TILE // 8, 8, TILE), axis=0))
        peak = jnp.max(peak, axis=0, keepdims=True)
        total = jnp.zeros((8, TILE), jnp.float32)
        inner = jnp.zeros((8, TILE), jnp.float32)
        for n in range(first, last + 1):
            at = slice(n * TILE, (n + 1) * TILE)
            g = lax.dot_general(
                v[at, :], do_i, (((1,), (1,)), ((), ())), preferred_element_type=jnp.float32
            )
            p = jnp.exp2(s_buf[at, :] - peak)
            s_buf[at, :] = p
            g_buf[at, :] = g
            total = total + jnp.sum(p.reshape(TILE // 8, 8, TILE), axis=0)
            inner = inner + jnp.sum((p * g).reshape(TILE // 8, 8, TILE), axis=0)
        inverse = 1.0 / jnp.sum(total, axis=0, keepdims=True)
        delta = jnp.sum(inner, axis=0, keepdims=True) * inverse
        scaled = inverse * SCORE_SCALE
        dq_t = jnp.zeros((HEAD_SIZE, TILE), jnp.float32)
        for n in range(first, last + 1):
            at = slice(n * TILE, (n + 1) * TILE)
            p = s_buf[at, :]
            mixed = ((p * scaled) * (g_buf[at, :] - delta)).astype(jnp.bfloat16)
            low = (p * inverse).astype(jnp.bfloat16)
            dv[at, :] += jnp.dot(low, do_i, preferred_element_type=jnp.float32)
            dk[at, :] += jnp.dot(mixed, q_i, preferred_element_type=jnp.float32)
            dq_t = dq_t + jnp.dot(kt[:, at], mixed, preferred_element_type=jnp.float32)
        dq[i * TILE : (i + 1) * TILE, :] = dq_t.T.astype(jnp.bfloat16)

    return tile


def scatter_kernel(
    spans, ka_count, dqh, dkh, dvh, dq, dk, dv, got, low, x_send, x_recv, q_send, q_recv, kv_send, kv_recv
):
    me = Place(spans, ka_count)
    tok = dq.shape[0]
    piece = dk.shape[0]
    me.greet()

    def exchange(ref):
        return pltpu.make_async_remote_copy(
            src_ref=ref,
            dst_ref=got,
            send_sem=x_send,
            recv_sem=x_recv,
            device_id=me.at(me.span, 2 * me.pair + 1 - me.core),
            device_id_type=MESH,
        )

    pl.when(me.core == 0)(lambda: exchange(dvh).start())
    pl.when(me.core == 1)(lambda: exchange(dkh).start())
    owner = 2 * me.pair + me.span // me.held
    cols = lanes(2 * (me.span % me.held) + me.core)
    for t in range(spans):
        span = (me.span + t) % spans
        src = dqh.at[rows_at(span * tok, tok), :]

        def remote(src=src, span=span):
            pltpu.make_async_remote_copy(
                src_ref=src,
                dst_ref=dq.at[:, cols],
                send_sem=q_send,
                recv_sem=q_recv,
                device_id=me.at(span, owner),
                device_id_type=MESH,
            ).start()

        if t == 0:
            pl.when(owner != me.ka)(remote)

            @pl.when(owner == me.ka)
            def _(src=src):
                pltpu.make_async_copy(src, dq.at[:, cols], q_recv).start()
        else:
            remote()
    wait_for(got, x_recv)
    for core, (own, out) in enumerate(((dkh, dk), (dvh, dv))):

        @pl.when(me.core == core)
        def _(own=own, out=out):
            low[...] = (own[...] + got[...]).astype(jnp.bfloat16)
            head_cols = lanes(me.head)
            for t in range(spans * ka_count):
                span = (me.span + t // ka_count) % spans
                ka = (me.ka + t % ka_count) % ka_count
                src = low.at[rows_at(span * tok + ka * piece, piece), :]
                dst = out.at[:, head_cols]
                if t == 0:
                    pltpu.make_async_copy(src, dst, kv_recv.at[core]).start()
                else:
                    pltpu.make_async_remote_copy(
                        src_ref=src,
                        dst_ref=dst,
                        send_sem=kv_send,
                        recv_sem=kv_recv.at[core],
                        device_id=me.at(span, ka),
                        device_id_type=MESH,
                    ).start()

    wait_for(got, x_send)
    sent = spans * tok
    pl.when(owner == me.ka)(lambda: wait_for(dqh.at[: sent - tok], q_send))
    pl.when(owner != me.ka)(lambda: wait_for(dqh.at[:sent], q_send))
    wait_for(dq, q_recv)
    wait_for(low.at[: (spans * ka_count - 1) * piece], kv_send)
    wait_for(dk, kv_recv.at[0])
    wait_for(dv, kv_recv.at[1])


def per_device(queries, output_gradient, key_states, value_inputs, turn_ids, listed):
    ka_count = lax.axis_size("ka")
    pb_count = lax.axis_size("pb")
    spans = 2 * KEY_VALUE_HEADS // ka_count
    groups = pb_count // spans
    tok = queries.shape[0]
    piece = key_states.shape[0]
    rows = spans * tok
    halo = rows
    bf16, f32 = jnp.bfloat16, jnp.float32
    any_space = pl.BlockSpec(memory_space=pl.ANY)
    vmem = pl.BlockSpec(memory_space=pltpu.VMEM)
    dma = pltpu.SemaphoreType.DMA
    head_rows = jax.ShapeDtypeStruct((rows, HEAD_SIZE), bf16)
    grads = [
        jax.ShapeDtypeStruct(queries.shape, bf16),
        jax.ShapeDtypeStruct(key_states.shape, bf16),
        jax.ShapeDtypeStruct(key_states.shape, bf16),
    ]
    low_rows = pltpu.VMEM((rows, HEAD_SIZE), bf16)
    full_rows = pltpu.VMEM((rows, HEAD_SIZE), f32)

    if groups == 1:
        out = pl.pallas_call(
            functools.partial(fused_kernel, spans, ka_count),
            out_shape=grads,
            in_specs=[pl.BlockSpec(memory_space=pltpu.SMEM), vmem]
            + [pl.BlockSpec(memory_space=pltpu.HBM)] * 4,
            out_specs=[any_space] * 3,
            scratch_shapes=[low_rows] * 4
            + [
                full_rows,
                pltpu.VMEM((HEAD_SIZE, rows), bf16),
                pltpu.VMEM((rows, TILE), f32),
                pltpu.VMEM((rows, TILE), f32),
                low_rows,
                full_rows,
                full_rows,
                full_rows,
                low_rows,
                dma,
                dma,
                dma((2,)),
                dma((2, spans)),
                dma,
                dma,
                dma,
                dma((spans,)),
                dma,
                dma,
                dma,
                dma((2,)),
            ],
            compiler_params=pltpu.CompilerParams(
                collective_id=2, has_side_effects=True, vmem_limit_bytes=FUSED_VMEM_LIMIT
            ),
            name="heads_backward",
        )(
            listed,
            turn_ids[None, :],
            queries,
            output_gradient,
            key_states,
            value_inputs,
        )
        return tuple(part.astype(f32) for part in out)

    q, do, k, v = pl.pallas_call(
        functools.partial(gather_kernel, spans, ka_count),
        out_shape=[head_rows] * 4,
        in_specs=[any_space] * 4,
        out_specs=[any_space] * 4,
        scratch_shapes=[dma, dma, dma((2,)), dma((2, spans)), dma, dma],
        compiler_params=pltpu.CompilerParams(collective_id=0, has_side_effects=True),
        name="gather_heads",
    )(queries, output_gradient, key_states, value_inputs)

    group = lax.axis_index("pb") // spans
    turn_own = lax.dynamic_slice_in_dim(turn_ids, group * rows, rows, 0)
    turn_before = lax.dynamic_slice_in_dim(turn_ids, jnp.maximum(group - 1, 0) * rows, rows, 0)
    turn_before = jnp.where(group > 0, turn_before, NO_KEY)
    turn_keys = jnp.concatenate([turn_before, turn_own])
    forward = [(i, i + spans) for i in range(pb_count - spans)]
    k_before, v_before = lax.ppermute(jnp.stack([k, v]), "pb", forward)
    k = jnp.concatenate([k_before, k])
    v = jnp.concatenate([v_before, v])
    keys = halo + rows
    key_grad = jax.ShapeDtypeStruct((keys, HEAD_SIZE), f32)
    dq, dk, dv = pl.pallas_call(
        functools.partial(attention_kernel, spans, ka_count, halo),
        out_shape=[head_rows, key_grad, key_grad],
        in_specs=[pl.BlockSpec(memory_space=pltpu.SMEM)] + [vmem] * 6,
        out_specs=[vmem] * 3,
        scratch_shapes=[
            pltpu.VMEM((HEAD_SIZE, keys), bf16),
            pltpu.VMEM((keys, TILE), f32),
            pltpu.VMEM((keys, TILE), f32),
        ],
        compiler_params=pltpu.CompilerParams(vmem_limit_bytes=VMEM_LIMIT),
        name="attention_backward",
    )(
        listed,
        turn_own.astype(f32)[None, :],
        jnp.broadcast_to(turn_keys.astype(f32)[:, None], (keys, HEAD_SIZE)),
        q,
        do,
        k,
        v,
    )
    back = [(i + spans, i) for i in range(pb_count - spans)]
    dk_later, dv_later = lax.ppermute(jnp.stack([dk[:halo], dv[:halo]]), "pb", back)
    dk = dk[halo:] + dk_later
    dv = dv[halo:] + dv_later

    out = pl.pallas_call(
        functools.partial(scatter_kernel, spans, ka_count),
        out_shape=grads,
        in_specs=[vmem] * 3,
        out_specs=[any_space] * 3,
        scratch_shapes=[
            pltpu.VMEM((rows, HEAD_SIZE), f32),
            pltpu.VMEM((rows, HEAD_SIZE), bf16),
            dma,
            dma,
            dma,
            dma,
            dma,
            dma((2,)),
        ],
        compiler_params=pltpu.CompilerParams(
            collective_id=1, has_side_effects=True, vmem_limit_bytes=VMEM_LIMIT
        ),
        name="scatter_gradients",
    )(dq, dk, dv)
    return tuple(part.astype(f32) for part in out)


def solution(mesh):
    in_specs = (
        P("pb", "ka"),
        P("pb", "ka"),
        P(("pb", "ka"), None),
        P(("pb", "ka"), None),
        P(),
        P(),
    )
    out_specs = (P("pb", "ka"), P(("pb", "ka"), None), P(("pb", "ka"), None))
    return jax.shard_map(
        per_device, mesh=mesh, in_specs=in_specs, out_specs=out_specs, check_vma=False
    )
```

```python
import functools

import jax
import jax.numpy as jnp
from jax import lax
from jax.experimental import pallas as pl
from jax.experimental.pallas import tpu as pltpu
from jax.sharding import PartitionSpec as P

QUERY_HEADS = 32
KEY_VALUE_HEADS = 16
HEAD_SIZE = 128
HEAD_GROUPS = 2
BLOCK_POSITIONS = 128
BACK = 14

SCORE_SCALE = 1.0 / 12.0
LOG2E = 1.4426950408889634
NEG_LARGE = -1e30
HIT = float(1 << 20)
NO_KEY = -(1 << 22)
TILE = 256
MESH = pl.DeviceIdType.MESH
VMEM_LIMIT = 48 * 1024 * 1024
FUSED_VMEM_LIMIT = 60 * 1024 * 1024


class Place:
    def __init__(self, spans, ka_count):
        self.spans = spans
        self.ka_count = ka_count
        pb = lax.axis_index("pb")
        self.ka = lax.axis_index("ka")
        self.group = pb // spans
        self.span = pb % spans
        self.pair = self.ka // 2
        self.core = self.ka % 2
        self.head = self.pair * spans + self.span
        self.held = KEY_VALUE_HEADS // ka_count

    def at(self, span, ka):
        return {"pb": self.group * self.spans + span, "ka": ka}

    def greet(self):
        barrier = pltpu.get_barrier_semaphore()
        for t in range(1, self.spans * self.ka_count):
            pl.semaphore_signal(
                barrier,
                inc=1,
                device_id=self.at(
                    (self.span + t // self.ka_count) % self.spans,
                    (self.ka + t % self.ka_count) % self.ka_count,
                ),
                device_id_type=MESH,
            )
        pl.semaphore_wait(barrier, self.spans * self.ka_count - 1)


def wait_for(ref, sem):
    pltpu.make_async_copy(ref, ref, sem).wait()


def lanes(index):
    return pl.ds(pl.multiple_of(index * HEAD_SIZE, HEAD_SIZE), HEAD_SIZE)


def rows_at(begin, count):
    return pl.ds(pl.multiple_of(begin, count), count)


def send_heads(me, q, do, k, v, qh, doh, kh, vh, kv_send, kv_recv, q_send, q_recv):
    tok = q.shape[0]
    piece = k.shape[0]
    kv_rows = rows_at(me.span * tok + me.ka * piece, piece)
    for t in range(me.spans * me.ka_count // 2):
        span = (me.span + t % me.spans) % me.spans
        pair = (me.pair + t // me.spans) % (me.ka_count // 2)
        cols = lanes(pair * me.spans + span)
        for core, (src, dst) in enumerate(((k, kh), (v, vh))):

            def remote(src=src, dst=dst, core=core, span=span, pair=pair, cols=cols):
                pltpu.make_async_remote_copy(
                    src_ref=src.at[:, cols],
                    dst_ref=dst.at[kv_rows, :],
                    send_sem=kv_send,
                    recv_sem=kv_recv,
                    device_id=me.at(span, 2 * pair + core),
                    device_id_type=MESH,
                ).start()

            if t == 0:
                pl.when(me.core != core)(remote)

                @pl.when(me.core == core)
                def _(src=src, dst=dst, cols=cols):
                    pltpu.make_async_copy(src.at[:, cols], dst.at[kv_rows, :], kv_recv).start()
            else:
                remote()
    q_rows = rows_at(me.span * tok, tok)
    for j in range(me.held):
        near = (me.span + j) % me.held
        span = me.held * me.core + near
        for core in range(2):
            cols = lanes(2 * near + core)
            mine = (span == me.span) & (me.core == core)
            for which, (src, dst) in enumerate(((q, qh), (do, doh))):
                sem = q_recv.at[which, me.span]

                @pl.when(mine)
                def _(src=src, dst=dst, cols=cols, sem=sem):
                    pltpu.make_async_copy(src.at[:, cols], dst.at[q_rows, :], sem).start()

                @pl.when(jnp.logical_not(mine))
                def _(src=src, dst=dst, cols=cols, core=core, span=span, which=which, sem=sem):
                    pltpu.make_async_remote_copy(
                        src_ref=src.at[:, cols],
                        dst_ref=dst.at[q_rows, :],
                        send_sem=q_send.at[which],
                        recv_sem=sem,
                        device_id=me.at(span, 2 * me.pair + core),
                        device_id_type=MESH,
                    ).start()


def to_other_core(me, src, dst, send_sem, recv_sem):
    return pltpu.make_async_remote_copy(
        src_ref=src,
        dst_ref=dst,
        send_sem=send_sem,
        recv_sem=recv_sem,
        device_id=me.at(me.span, 2 * me.pair + 1 - me.core),
        device_id_type=MESH,
    )


def share_keys(me, kh, vh, kv_recv, x_send, x_recv):
    for core, ref in enumerate((kh, vh)):

        @pl.when(me.core == core)
        def _(ref=ref):
            wait_for(ref, kv_recv)
            to_other_core(me, ref, ref, x_send, x_recv).start()

    wait_for(kh, x_recv)


def finish_heads(me, qh, doh, kh, kv_send, q_send, x_send, tok, piece):
    wait_for(kh, x_send)
    wait_for(kh.at[: (me.spans * me.ka_count - 1) * piece], kv_send)
    sent = 2 * me.held * tok
    has_own = me.span // me.held == me.core
    for which, ref in enumerate((qh, doh)):
        sem = q_send.at[which]
        pl.when(has_own)(lambda ref=ref, sem=sem: wait_for(ref.at[: sent - tok], sem))
        pl.when(jnp.logical_not(has_own))(lambda ref=ref, sem=sem: wait_for(ref.at[:sent], sem))


def gather_kernel(
    spans, ka_count, q, do, k, v, qh, doh, kh, vh, kv_send, kv_recv, q_send, q_recv, x_send, x_recv
):
    me = Place(spans, ka_count)
    tok = q.shape[0]
    me.greet()
    send_heads(me, q, do, k, v, qh, doh, kh, vh, kv_send, kv_recv, q_send, q_recv)
    share_keys(me, kh, vh, kv_recv, x_send, x_recv)
    for span in range(spans):
        wait_for(qh.at[span * tok : (span + 1) * tok], q_recv.at[0, span])
        wait_for(doh.at[span * tok : (span + 1) * tok], q_recv.at[1, span])
    finish_heads(me, qh, doh, kh, kv_send, q_send, x_send, tok, k.shape[0])


def fused_kernel(
    spans, ka_count, listed, turn_row, q, do, k, v, dq, dk, dv,
    qh, doh, kh, vh, turn_col, kt, s_buf, g_buf, dqh, dkh, dvh, got, low,
    kv_send, kv_recv, q_send, q_recv, k_send, k_recv,
    x_send, x_recv, dq_send, dq_recv, dkv_send, dkv_recv,
):
    me = Place(spans, ka_count)
    tok = q.shape[0]
    piece = k.shape[0]
    me.greet()
    send_heads(me, q, do, k, v, qh, doh, kh, vh, kv_send, kv_recv, q_send, q_recv)
    for n in range(turn_col.shape[0] // HEAD_SIZE):
        at = slice(n * HEAD_SIZE, (n + 1) * HEAD_SIZE)
        turns = turn_row[:, at].astype(jnp.float32)
        turn_col[at, :] = jnp.broadcast_to(turns, (HEAD_SIZE, HEAD_SIZE)).T
    share_keys(me, kh, vh, kv_recv, k_send, k_recv)
    owner = 2 * me.pair + me.span // me.held
    q_cols = lanes(2 * (me.span % me.held) + me.core)
    head_cols = lanes(me.head)

    def ready(span):
        for which, ref in enumerate((qh, doh)):
            wait_for(ref.at[rows_at(span * tok, tok), :], q_recv.at[which, span])

    def send_queries(span):
        src = dqh.at[rows_at(span * tok, tok), :]
        mine = (me.span == span) & (owner == me.ka)

        @pl.when(mine)
        def _():
            pltpu.make_async_copy(src, dq.at[:, q_cols], dq_recv).start()

        @pl.when(jnp.logical_not(mine))
        def _():
            pltpu.make_async_remote_copy(
                src_ref=src,
                dst_ref=dq.at[:, q_cols],
                send_sem=dq_send,
                recv_sem=dq_recv,
                device_id=me.at(span, owner),
                device_id_type=MESH,
            ).start()

    tile = attend(me, 0, listed, turn_row, turn_col, qh, doh, kh, vh, dqh, dkh, dvh, kt, s_buf, g_buf)

    def query_step(t, carry):
        span = (me.span + me.held - t // 2) % me.held
        span = span + me.held * ((t + me.span // me.held) % 2)
        ready(span)
        for i in range(spans):
            pl.when(span == i)(functools.partial(tile, i))
        send_queries(span)
        return carry

    lax.fori_loop(0, spans, query_step, 0)

    def share_step(t, carry):
        span = (me.span + t) % spans
        at = rows_at(span * tok, tok)
        for core, ref in enumerate((dvh, dkh)):

            @pl.when(me.core == core)
            def _(ref=ref):
                to_other_core(
                    me, ref.at[at, :], got.at[at, :], x_send, x_recv.at[span]
                ).start()

        return carry

    lax.fori_loop(0, spans, share_step, 0)

    def grad_step(t, carry):
        span = (me.span + t) % spans
        at = rows_at(span * tok, tok)
        wait_for(got.at[at, :], x_recv.at[span])
        for core, (own, out) in enumerate(((dkh, dk), (dvh, dv))):

            @pl.when(me.core == core)
            def _(own=own, out=out, core=core):
                low[at, :] = (own[at, :] + got[at, :]).astype(jnp.bfloat16)
                dst = out.at[:, head_cols]
                for n in range(ka_count):
                    ka = (me.ka + n) % ka_count
                    src = low.at[rows_at(span * tok + ka * piece, piece), :]

                    def remote(src=src, ka=ka):
                        pltpu.make_async_remote_copy(
                            src_ref=src,
                            dst_ref=dst,
                            send_sem=dkv_send,
                            recv_sem=dkv_recv.at[core],
                            device_id=me.at(span, ka),
                            device_id_type=MESH,
                        ).start()

                    if n == 0:
                        pl.when(me.span != span)(remote)

                        @pl.when(me.span == span)
                        def _(src=src):
                            pltpu.make_async_copy(src, dst, dkv_recv.at[core]).start()
                    else:
                        remote()

        return carry

    lax.fori_loop(0, spans, grad_step, 0)
    finish_heads(me, qh, doh, kh, kv_send, q_send, k_send, tok, piece)
    wait_for(got, x_send)
    sent = spans * tok
    pl.when(owner == me.ka)(lambda: wait_for(dqh.at[: sent - tok], dq_send))
    pl.when(owner != me.ka)(lambda: wait_for(dqh.at[:sent], dq_send))
    wait_for(low.at[: (spans * ka_count - 1) * piece], dkv_send)
    wait_for(dq, dq_recv)
    wait_for(dk, dkv_recv.at[0])
    wait_for(dv, dkv_recv.at[1])


def attention_kernel(spans, ka_count, halo, *refs):
    tile = attend(Place(spans, ka_count), halo, *refs)
    for i in range(refs[3].shape[0] // TILE):
        tile(i)


def attend(me, halo, listed, turn_row, turn_col, q, do, k, v, dq, dk, dv, kt, s_buf, g_buf):
    rows = q.shape[0]
    keys = k.shape[0]
    head_group = me.head // (KEY_VALUE_HEADS // HEAD_GROUPS)
    block_base = me.group * (rows // BLOCK_POSITIONS)
    dk[...] = jnp.zeros_like(dk)
    dv[...] = jnp.zeros_like(dv)
    for n in range(keys // TILE):
        kt[:, n * TILE : (n + 1) * TILE] = k[n * TILE : (n + 1) * TILE, :].T
    left = lax.broadcasted_iota(jnp.int32, (1, TILE), 1) < BLOCK_POSITIONS
    causal = lax.broadcasted_iota(jnp.int32, (TILE, TILE), 0) <= lax.broadcasted_iota(
        jnp.int32, (TILE, TILE), 1
    )

    def hit(block, key_block):
        offset = block - key_block - 1
        if 0 <= offset < BACK:
            return listed[offset, head_group, block_base + block]
        return jnp.int32(0)

    def tile(i):
        q_i = q[i * TILE : (i + 1) * TILE, :]
        do_i = do[i * TILE : (i + 1) * TILE, :]
        turn_i = turn_row[:, i * TILE : (i + 1) * TILE].astype(jnp.float32)
        last = halo // TILE + i
        first = max(0, last - BACK * BLOCK_POSITIONS // TILE)
        peak = jnp.full((8, TILE), NEG_LARGE, jnp.float32)
        for n in range(first, last + 1):
            at = slice(n * TILE, (n + 1) * TILE)
            s = lax.dot_general(
                k[at, :], q_i, (((1,), (1,)), ((), ())), preferred_element_type=jnp.float32
            ) * (SCORE_SCALE * LOG2E)
            parts = []
            for half in range(TILE // BLOCK_POSITIONS):
                key_block = 2 * n + half - halo // BLOCK_POSITIONS
                seen = jnp.where(left, hit(2 * i, key_block), hit(2 * i + 1, key_block))
                bar = turn_i - seen.astype(jnp.float32) * HIT
                begin = n * TILE + half * BLOCK_POSITIONS
                turns = turn_col[begin : begin + BLOCK_POSITIONS, :]
                parts.append(jnp.concatenate([turns, turns], axis=1) >= bar)
            allowed = jnp.concatenate(parts, axis=0)
            if n == last:
                allowed = allowed & causal
            s = jnp.where(allowed, s, NEG_LARGE)
            s_buf[at, :] = s
            peak = jnp.maximum(peak, jnp.max(s.reshape(TILE // 8, 8, TILE), axis=0))
        peak = jnp.max(peak, axis=0, keepdims=True)
        total = jnp.zeros((8, TILE), jnp.float32)
        inner = jnp.zeros((8, TILE), jnp.float32)
        for n in range(first, last + 1):
            at = slice(n * TILE, (n + 1) * TILE)
            g = lax.dot_general(
                v[at, :], do_i, (((1,), (1,)), ((), ())), preferred_element_type=jnp.float32
            )
            p = jnp.exp2(s_buf[at, :] - peak)
            s_buf[at, :] = p
            g_buf[at, :] = g
            total = total + jnp.sum(p.reshape(TILE // 8, 8, TILE), axis=0)
            inner = inner + jnp.sum((p * g).reshape(TILE // 8, 8, TILE), axis=0)
        inverse = 1.0 / jnp.sum(total, axis=0, keepdims=True)
        delta = jnp.sum(inner, axis=0, keepdims=True) * inverse
        scaled = inverse * SCORE_SCALE
        dq_t = jnp.zeros((HEAD_SIZE, TILE), jnp.float32)
        for n in range(first, last + 1):
            at = slice(n * TILE, (n + 1) * TILE)
            p = s_buf[at, :]
            mixed = ((p * scaled) * (g_buf[at, :] - delta)).astype(jnp.bfloat16)
            low = (p * inverse).astype(jnp.bfloat16)
            dv[at, :] += jnp.dot(low, do_i, preferred_element_type=jnp.float32)
            dk[at, :] += jnp.dot(mixed, q_i, preferred_element_type=jnp.float32)
            dq_t = dq_t + jnp.dot(kt[:, at], mixed, preferred_element_type=jnp.float32)
        dq[i * TILE : (i + 1) * TILE, :] = dq_t.T.astype(jnp.bfloat16)

    return tile


def scatter_kernel(
    spans, ka_count, dqh, dkh, dvh, dq, dk, dv, got, low, x_send, x_recv, q_send, q_recv, kv_send, kv_recv
):
    me = Place(spans, ka_count)
    tok = dq.shape[0]
    piece = dk.shape[0]
    me.greet()

    def exchange(ref):
        return pltpu.make_async_remote_copy(
            src_ref=ref,
            dst_ref=got,
            send_sem=x_send,
            recv_sem=x_recv,
            device_id=me.at(me.span, 2 * me.pair + 1 - me.core),
            device_id_type=MESH,
        )

    pl.when(me.core == 0)(lambda: exchange(dvh).start())
    pl.when(me.core == 1)(lambda: exchange(dkh).start())
    owner = 2 * me.pair + me.span // me.held
    cols = lanes(2 * (me.span % me.held) + me.core)
    for t in range(spans):
        span = (me.span + t) % spans
        src = dqh.at[rows_at(span * tok, tok), :]

        def remote(src=src, span=span):
            pltpu.make_async_remote_copy(
                src_ref=src,
                dst_ref=dq.at[:, cols],
                send_sem=q_send,
                recv_sem=q_recv,
                device_id=me.at(span, owner),
                device_id_type=MESH,
            ).start()

        if t == 0:
            pl.when(owner != me.ka)(remote)

            @pl.when(owner == me.ka)
            def _(src=src):
                pltpu.make_async_copy(src, dq.at[:, cols], q_recv).start()
        else:
            remote()
    wait_for(got, x_recv)
    for core, (own, out) in enumerate(((dkh, dk), (dvh, dv))):

        @pl.when(me.core == core)
        def _(own=own, out=out):
            low[...] = (own[...] + got[...]).astype(jnp.bfloat16)
            head_cols = lanes(me.head)
            for t in range(spans * ka_count):
                span = (me.span + t // ka_count) % spans
                ka = (me.ka + t % ka_count) % ka_count
                src = low.at[rows_at(span * tok + ka * piece, piece), :]
                dst = out.at[:, head_cols]
                if t == 0:
                    pltpu.make_async_copy(src, dst, kv_recv.at[core]).start()
                else:
                    pltpu.make_async_remote_copy(
                        src_ref=src,
                        dst_ref=dst,
                        send_sem=kv_send,
                        recv_sem=kv_recv.at[core],
                        device_id=me.at(span, ka),
                        device_id_type=MESH,
                    ).start()

    wait_for(got, x_send)
    sent = spans * tok
    pl.when(owner == me.ka)(lambda: wait_for(dqh.at[: sent - tok], q_send))
    pl.when(owner != me.ka)(lambda: wait_for(dqh.at[:sent], q_send))
    wait_for(dq, q_recv)
    wait_for(low.at[: (spans * ka_count - 1) * piece], kv_send)
    wait_for(dk, kv_recv.at[0])
    wait_for(dv, kv_recv.at[1])


def widen_kernel(*refs):
    for src, dst in zip(refs[:3], refs[3:]):
        dst[...] = src[...].astype(jnp.float32)


def widen(parts):
    steps = 4
    blocks = [pl.BlockSpec((p.shape[0] // steps, p.shape[1]), lambda i: (i, 0)) for p in parts]
    return tuple(
        pl.pallas_call(
            widen_kernel,
            grid=(steps,),
            out_shape=[jax.ShapeDtypeStruct(p.shape, jnp.float32) for p in parts],
            in_specs=blocks,
            out_specs=blocks,
            compiler_params=pltpu.CompilerParams(vmem_limit_bytes=FUSED_VMEM_LIMIT),
            name="widen_gradients",
        )(*parts)
    )


def per_device(queries, output_gradient, key_states, value_inputs, turn_ids, listed):
    ka_count = lax.axis_size("ka")
    pb_count = lax.axis_size("pb")
    spans = 2 * KEY_VALUE_HEADS // ka_count
    groups = pb_count // spans
    tok = queries.shape[0]
    piece = key_states.shape[0]
    rows = spans * tok
    halo = rows
    bf16, f32 = jnp.bfloat16, jnp.float32
    any_space = pl.BlockSpec(memory_space=pl.ANY)
    vmem = pl.BlockSpec(memory_space=pltpu.VMEM)
    dma = pltpu.SemaphoreType.DMA
    head_rows = jax.ShapeDtypeStruct((rows, HEAD_SIZE), bf16)
    grads = [
        jax.ShapeDtypeStruct(queries.shape, bf16),
        jax.ShapeDtypeStruct(key_states.shape, bf16),
        jax.ShapeDtypeStruct(key_states.shape, bf16),
    ]
    low_rows = pltpu.VMEM((rows, HEAD_SIZE), bf16)
    full_rows = pltpu.VMEM((rows, HEAD_SIZE), f32)

    if groups == 1:
        out = pl.pallas_call(
            functools.partial(fused_kernel, spans, ka_count),
            out_shape=grads,
            in_specs=[pl.BlockSpec(memory_space=pltpu.SMEM), vmem]
            + [pl.BlockSpec(memory_space=pltpu.HBM)] * 4,
            out_specs=[any_space] * 3,
            scratch_shapes=[low_rows] * 4
            + [
                full_rows,
                pltpu.VMEM((HEAD_SIZE, rows), bf16),
                pltpu.VMEM((rows, TILE), f32),
                pltpu.VMEM((rows, TILE), f32),
                low_rows,
                full_rows,
                full_rows,
                full_rows,
                low_rows,
                dma,
                dma,
                dma((2,)),
                dma((2, spans)),
                dma,
                dma,
                dma,
                dma((spans,)),
                dma,
                dma,
                dma,
                dma((2,)),
            ],
            compiler_params=pltpu.CompilerParams(
                collective_id=2, has_side_effects=True, vmem_limit_bytes=FUSED_VMEM_LIMIT
            ),
            name="heads_backward",
        )(
            jnp.transpose(listed, (2, 0, 1)),
            turn_ids[None, :],
            queries,
            output_gradient,
            key_states,
            value_inputs,
        )
        return widen(out)

    q, do, k, v = pl.pallas_call(
        functools.partial(gather_kernel, spans, ka_count),
        out_shape=[head_rows] * 4,
        in_specs=[any_space] * 4,
        out_specs=[any_space] * 4,
        scratch_shapes=[dma, dma, dma((2,)), dma((2, spans)), dma, dma],
        compiler_params=pltpu.CompilerParams(collective_id=0, has_side_effects=True),
        name="gather_heads",
    )(queries, output_gradient, key_states, value_inputs)

    group = lax.axis_index("pb") // spans
    turn_own = lax.dynamic_slice_in_dim(turn_ids, group * rows, rows, 0)
    turn_before = lax.dynamic_slice_in_dim(turn_ids, jnp.maximum(group - 1, 0) * rows, rows, 0)
    turn_before = jnp.where(group > 0, turn_before, NO_KEY)
    turn_keys = jnp.concatenate([turn_before, turn_own])
    forward = [(i, i + spans) for i in range(pb_count - spans)]
    k_before, v_before = lax.ppermute(jnp.stack([k, v]), "pb", forward)
    k = jnp.concatenate([k_before, k])
    v = jnp.concatenate([v_before, v])
    keys = halo + rows
    key_grad = jax.ShapeDtypeStruct((keys, HEAD_SIZE), f32)
    dq, dk, dv = pl.pallas_call(
        functools.partial(attention_kernel, spans, ka_count, halo),
        out_shape=[head_rows, key_grad, key_grad],
        in_specs=[pl.BlockSpec(memory_space=pltpu.SMEM)] + [vmem] * 6,
        out_specs=[vmem] * 3,
        scratch_shapes=[
            pltpu.VMEM((HEAD_SIZE, keys), bf16),
            pltpu.VMEM((keys, TILE), f32),
            pltpu.VMEM((keys, TILE), f32),
        ],
        compiler_params=pltpu.CompilerParams(vmem_limit_bytes=VMEM_LIMIT),
        name="attention_backward",
    )(
        jnp.transpose(listed, (2, 0, 1)),
        turn_own.astype(f32)[None, :],
        jnp.broadcast_to(turn_keys.astype(f32)[:, None], (keys, HEAD_SIZE)),
        q,
        do,
        k,
        v,
    )
    back = [(i + spans, i) for i in range(pb_count - spans)]
    dk_later, dv_later = lax.ppermute(jnp.stack([dk[:halo], dv[:halo]]), "pb", back)
    dk = dk[halo:] + dk_later
    dv = dv[halo:] + dv_later

    out = pl.pallas_call(
        functools.partial(scatter_kernel, spans, ka_count),
        out_shape=grads,
        in_specs=[vmem] * 3,
        out_specs=[any_space] * 3,
        scratch_shapes=[
            pltpu.VMEM((rows, HEAD_SIZE), f32),
            pltpu.VMEM((rows, HEAD_SIZE), bf16),
            dma,
            dma,
            dma,
            dma,
            dma,
            dma((2,)),
        ],
        compiler_params=pltpu.CompilerParams(
            collective_id=1, has_side_effects=True, vmem_limit_bytes=VMEM_LIMIT
        ),
        name="scatter_gradients",
    )(dq, dk, dv)
    return widen(out)


def solution(mesh):
    in_specs = (
        P("pb", "ka"),
        P("pb", "ka"),
        P(("pb", "ka"), None),
        P(("pb", "ka"), None),
        P(),
        P(),
    )
    out_specs = (P("pb", "ka"), P(("pb", "ka"), None), P(("pb", "ka"), None))
    return jax.shard_map(
        per_device, mesh=mesh, in_specs=in_specs, out_specs=out_specs, check_vma=False
    )
```
